768 devices in a mesh: group: 8 (over y_hi, core), inner: 96 (over z, y_lo, x).
Axes of the slice: x: 4, y: 8 (y_hi: 4, y_lo: 2; y = y_hi * 2 + y_lo), z: 12, core: 2. Of those that a mesh axis runs over, the one named last changes fastest.
Arguments:
- hidden_in: bfloat16 [98304, 8192], P(('group', 'inner')), may hold values from -6 to 6
- cotangent: bfloat16 [98304, 128], P(('group', 'inner')), may hold values from -6 to 6
- params: bfloat16 [96, 11008], P('inner', 'group'), may hold values from -1 to 2, as said below
Outputs:
- key_rows: bfloat16 [98304, 128], P(('group', 'inner'))
- input_grad: bfloat16 [98304, 8192], P(('group', 'inner'))
- param_grad: float32 [96, 11008], P('inner', 'group')
The draws below stay inside these ranges and needn't reach their ends.
Inputs may be any that keep to these rules, and one draw needn't show every extreme that they name: `params`: the first 1048576 entries of the flat vector are weights of order 8192 ** -0.5, the last 8192 are gains near one.
All inputs are finite; a program needn't handle non-finite values.
Results may differ from the reference program's by a relative error of at most 0.017.
Values may be sent and summed in bfloat16 or wider, within the bound.
No kernel may reach another device: no remote copies, remote signals or barrier semaphores. Data moves between devices by JAX's collectives and lax.ppermute only.
A program may use at most 64 MiB of HBM per device.

```python
import jax
import jax.numpy as jnp
from jax import lax

D = 8192
HD = 128
TOK_DEV = 128
TOKENS = 98304
PARAMS = 1056768
N_GROUP = 8
N_INNER = 96


def draw_params(key, part):
    key = jax.random.fold_in(key, 7)
    key_weight, key_gain = jax.random.split(key)
    weights = jax.random.normal(key_weight, (D * HD,), jnp.float32) * D ** (-0.5)
    gains = 1.0 + 0.1 * jnp.clip(jax.random.normal(key_gain, (D,), jnp.float32), -4.0, 4.0)
    flat_params = jnp.concatenate([weights, gains])
    return flat_params.astype(jnp.bfloat16).reshape(N_INNER, PARAMS // N_INNER)


def block_scale(key, extent, cuts, smallest, high):
    gain, own = 1.0, jax.random.fold_in(key, 6)
    for axis_at, parts in cuts:
        heights = jnp.exp(jax.random.uniform(jax.random.fold_in(own, axis_at), (parts,), jnp.float32, smallest / len(cuts), high / len(cuts)))
        gain = gain * jnp.repeat(heights, extent[axis_at] // parts).reshape([-1 if axis == axis_at else 1 for axis in range(len(extent))])
    return gain


def bell_draw(key, shape, spread, limit, cuts=(), held_as=jnp.bfloat16):
    level = block_scale(key, shape, cuts, -0.22, 0.18) if cuts else 1.0
    entries = jax.random.normal(key, shape, jnp.float32) * spread * level
    return jnp.minimum(jnp.maximum(entries, -limit), limit).astype(held_as)


def setup_inputs(seed: int = 0) -> dict:
    streams_of = jax.random.split(jax.random.key(seed), 4)
    return {
        "hidden_in": bell_draw(streams_of[0], (TOKENS, D), 1.0, 6.0, ((0, 768),)),
        "cotangent": bell_draw(streams_of[1], (TOKENS, HD), 1.0, 6.0, ((0, 768),)),
        "params": draw_params(jax.random.fold_in(streams_of[3], 71), 0),
    }


def reference(hidden_in, cotangent, params):
    flat_params = params.reshape(-1)
    weight = flat_params[:D * HD].reshape(D, HD)
    norm_gain = flat_params[D * HD:].astype(jnp.float32)
    block_rows = TOK_DEV * N_GROUP
    blocks = TOKENS // block_rows
    inputs_blocked = hidden_in.reshape(blocks, block_rows, D)
    cotan_blocked = cotangent.reshape(blocks, block_rows, HD)

    def one_block(carry, pieces):
        weight_sum, gain_sum = carry
        rows_in, rows_cot = pieces
        inputs32 = rows_in.astype(jnp.float32)
        inv_rms = lax.rsqrt(lax.optimization_barrier(jnp.mean(inputs32 * inputs32, axis=-1, keepdims=True)) + 1e-05)
        normed = inputs32 * inv_rms
        normed_rows = (normed * norm_gain).astype(jnp.bfloat16)
        key_block = jnp.dot(normed_rows, weight, preferred_element_type=jnp.float32).astype(jnp.bfloat16)
        back_proj = jnp.dot(rows_cot, weight.T, preferred_element_type=jnp.float32)
        norm_back = back_proj * norm_gain
        grad_block = (inv_rms * (norm_back - normed * lax.optimization_barrier(jnp.mean(norm_back * normed, axis=-1, keepdims=True)))).astype(jnp.bfloat16)
        weight_sum = weight_sum + jnp.dot(normed_rows.T, rows_cot, preferred_element_type=jnp.float32)
        gain_sum = gain_sum + lax.optimization_barrier(jnp.sum(back_proj * normed, axis=0))
        return ((weight_sum, gain_sum), (key_block, grad_block))
    start = (jnp.zeros((D, HD), jnp.float32), jnp.zeros((D,), jnp.float32))
    (weight_grad, gain_grad), (key_parts, grad_parts) = lax.scan(one_block, start, (inputs_blocked, cotan_blocked))
    key_rows = key_parts.reshape(TOKENS, HD)
    input_grad = grad_parts.reshape(TOKENS, D)
    param_grad = jnp.concatenate([weight_grad.reshape(-1), gain_grad]).reshape(params.shape)
    return (key_rows, input_grad, param_grad)
```

```python
import jax
import jax.numpy as jnp
from jax import lax
from jax.experimental import pallas as pl
from jax.experimental.pallas import tpu as pltpu
from jax.sharding import Mesh, PartitionSpec as P

AXES = ("yh", "c", "z", "yl", "x")
SIZES = (4, 2, 12, 2, 4)
ZY = ("z", "yh", "yl")
N_ZY = 96

LANES = 128
BLK = 16
USED = 12
GROUP_ROWS = 86
PIECE = 1376
EPS = 1e-05
ROWS_PAD = 8272
STEP = 512


def swap(a):
    return lax.ppermute(a, "c", [(0, 1), (1, 0)])


def shift_x(a, k):
    return lax.ppermute(a, "x", [(i, (i + k) % 4) for i in range(4)])


def sums_kernel(pos_ref, hidden_ref, cot_ref, own_ref, send_ref, inv_ref, u_ref):
    width = hidden_ref.shape[1]
    x, c = pos_ref[0], pos_ref[1]

    def squares(m, acc):
        part = hidden_ref[:, pl.ds(pl.multiple_of(m * STEP, STEP), STEP)].astype(jnp.float32)
        part = part * part
        for k in range(STEP // LANES):
            acc = acc + part[:, k * LANES : (k + 1) * LANES]
        return acc

    acc = lax.fori_loop(0, width // STEP, squares, jnp.zeros((hidden_ref.shape[0], LANES), jnp.float32))
    inv = lax.rsqrt(jnp.sum(acc, axis=1, keepdims=True) / width + EPS)
    inv_ref[...] = jnp.broadcast_to(inv, inv_ref.shape)
    cots = (cot_ref[...].astype(jnp.float32) * inv).astype(jnp.bfloat16)

    def outer(m, _):
        at = pl.multiple_of(m * STEP, STEP)
        u_ref[pl.ds(at, STEP), :] = lax.dot_general(
            hidden_ref[:, pl.ds(at, STEP)], cots, (((0,), (0,)), ((), ())), preferred_element_type=jnp.float32
        )
        return 0

    lax.fori_loop(0, width // STEP, outer, 0)
    u_ref[width:, :] = jnp.zeros((ROWS_PAD - width, LANES), jnp.float32)

    def pack(q, _):
        for k in range(4):
            base = GROUP_ROWS * (q * 4 + lax.rem(x + k, 4))
            for yh in range(4):
                at = (q // 2) * 8 + yh * 2 + lax.rem(q, 2)
                for out, core in ((own_ref, c), (send_ref, 1 - c)):
                    row = base + lax.div(43 * (2 * yh + core), 4)
                    out[k, at] = u_ref[pl.ds(row, BLK), :].astype(jnp.bfloat16)
        return 0

    lax.fori_loop(0, 24, pack, 0)


def rows_kernel(pos_ref, hidden_ref, cot_ref, inv_ref, *refs):
    pieces = (refs[:4], refs[4:8])
    key_ref, grad_ref, gain_ref, s_ref, w_ref = refs[8:]
    width = hidden_ref.shape[1]
    x, c = pos_ref[0], pos_ref[1]

    s_ref[1, 0:BLK, :] = jnp.zeros((BLK, LANES), jnp.float32)
    tail = jnp.zeros((22 - BLK, LANES), jnp.float32)
    one = jnp.zeros((1, LANES), jnp.float32)

    def assemble(q, _):
        for k in range(4):
            base = GROUP_ROWS * (q * 4 + lax.rem(x + 4 - k, 4))
            for core, group in ((c, pieces[0]), (1 - c, pieces[1])):
                s_ref[core, pl.ds(base + 85, 1), :] = one
                for yh in range(4):
                    at = (q // 2) * 8 + yh * 2 + lax.rem(q, 2)
                    row = base + lax.div(43 * (2 * yh + core), 4)
                    s_ref[core, pl.ds(row, BLK), :] = group[k][at].astype(jnp.float32)
                    rest = 6 if yh < 3 else 5
                    s_ref[core, pl.ds(row + BLK, rest), :] = tail[:rest]
        return 0

    lax.fori_loop(0, 24, assemble, 0)
    gain_ref[...] = s_ref[0, width : width + 64, :] + s_ref[1, width : width + 64, :]
    inv = inv_ref[...]

    def forward(m, key):
        at = pl.multiple_of(m * STEP, STEP)
        weight = (s_ref[0, pl.ds(at, STEP), :] + s_ref[1, pl.ds(at, STEP), :]).astype(jnp.bfloat16)
        w_ref[pl.ds(at, STEP), :] = weight
        rows = []
        for k in range(STEP // LANES):
            part = hidden_ref[:, pl.ds(pl.multiple_of(at + k * LANES, LANES), LANES)].astype(jnp.float32)
            gain = gain_ref[pl.ds(m * (STEP // LANES) + k, 1), :]
            rows.append((part * inv * gain).astype(jnp.bfloat16))
        return key + jnp.dot(jnp.concatenate(rows, axis=1), weight, preferred_element_type=jnp.float32)

    key = lax.fori_loop(0, width // STEP, forward, jnp.zeros(key_ref.shape, jnp.float32))
    key_ref[...] = key.astype(jnp.bfloat16)
    cot = cot_ref[...]
    scale = inv * (jnp.sum(cot.astype(jnp.float32) * key, axis=1, keepdims=True) / width)

    def backward(m, _):
        at = pl.multiple_of(m * STEP, STEP)
        back = lax.dot_general(
            cot, w_ref[pl.ds(at, STEP), :], (((1,), (1,)), ((), ())), preferred_element_type=jnp.float32
        )
        for k in range(STEP // LANES):
            lanes = pl.ds(pl.multiple_of(at + k * LANES, LANES), LANES)
            part = hidden_ref[:, lanes].astype(jnp.float32)
            gain = gain_ref[pl.ds(m * (STEP // LANES) + k, 1), :]
            grad = inv * (back[:, k * LANES : (k + 1) * LANES] * gain - part * scale)
            grad_ref[:, lanes] = grad.astype(jnp.bfloat16)
        return 0

    lax.fori_loop(0, width // STEP, backward, 0)


def local(hidden_in, cotangent, params):
    tokens, width = hidden_in.shape
    x, c, z = lax.axis_index("x"), lax.axis_index("c"), lax.axis_index("z")
    yh, yl = lax.axis_index("yh"), lax.axis_index("yl")
    inner, j = (z * 2 + yl) * 4 + x, yh * 2 + c
    first_row, lane = (43 * j) // 4, (96 * j) % LANES
    pos = jnp.stack([x, c]).astype(jnp.int32)
    smem = pl.BlockSpec(memory_space=pltpu.SMEM)
    vmem = pl.BlockSpec(memory_space=pltpu.VMEM)
    bf16, f32 = jnp.bfloat16, jnp.float32

    flat = jnp.pad(params.reshape(-1), (LANES, BLK * LANES - PIECE))
    block = lax.dynamic_slice(flat, (LANES - lane,), (BLK * LANES,)).reshape(1, BLK, LANES)
    mine = lax.all_to_all(jnp.broadcast_to(block, (N_ZY, BLK, LANES)), ZY, 0, 0, tiled=True)

    half = jax.ShapeDtypeStruct((4, N_ZY, BLK, LANES), bf16)
    own, send, inv = pl.pallas_call(
        sums_kernel,
        out_shape=(half, half, jax.ShapeDtypeStruct((tokens, LANES), f32)),
        in_specs=[smem, vmem, vmem],
        out_specs=(vmem, vmem, vmem),
        scratch_shapes=[pltpu.VMEM((ROWS_PAD, LANES), f32)],
        compiler_params=pltpu.CompilerParams(vmem_limit_bytes=24 << 20),
        cost_estimate=pl.CostEstimate(flops=4 * tokens * width * LANES, bytes_accessed=8 << 20, transcendentals=0),
    )(pos, hidden_in, cotangent)
    got = swap(send)
    pair = [own[k].astype(f32) + got[k].astype(f32) for k in range(4)]
    moved = [shift_x(pair[k].astype(bf16), k) for k in range(1, 4)]

    held = [mine] + [shift_x(mine, k) for k in range(1, 4)]
    other = [swap(a) for a in held]

    total = pair[0] + moved[0].astype(f32) + moved[1].astype(f32) + moved[2].astype(f32)
    gain_part = jnp.sum(mine.astype(f32) * total, axis=-1)[:, :USED].reshape(12, 8 * USED)
    pays = [jnp.zeros((512,), f32)]
    for start in (0, 3, 7):
        pays.append(jnp.pad(gain_part[start : start + 5].reshape(-1), (0, 32)))
    pay = jnp.stack(pays).reshape(4, 1, 4, LANES)
    pay = jnp.concatenate([jnp.zeros_like(pay), pay], axis=1).reshape(8, 4, LANES)
    pay = jnp.pad(pay, ((N_ZY - 8, 0), (USED, 0), (0, 0)))
    spare = lax.broadcasted_iota(jnp.int32, (1, BLK, 1), 1) >= USED
    chunk = jnp.where(spare, pay, total).astype(bf16)
    sums = lax.all_to_all(chunk, ZY, 0, 0, tiled=True).astype(f32).sum(axis=0)

    key_rows, input_grad, gains = pl.pallas_call(
        rows_kernel,
        out_shape=(
            jax.ShapeDtypeStruct((tokens, LANES), bf16),
            jax.ShapeDtypeStruct((tokens, width), bf16),
            jax.ShapeDtypeStruct((64, LANES), f32),
        ),
        in_specs=[smem] + [vmem] * 11,
        out_specs=(vmem, vmem, vmem),
        scratch_shapes=[pltpu.VMEM((2, ROWS_PAD, LANES), f32), pltpu.VMEM((width, LANES), bf16)],
        compiler_params=pltpu.CompilerParams(vmem_limit_bytes=36 << 20),
        cost_estimate=pl.CostEstimate(flops=4 * tokens * width * LANES, bytes_accessed=10 << 20, transcendentals=0),
    )(pos, hidden_in, cotangent, inv, *held, *other)

    part = sums[USED:]
    parts = jnp.stack([shift_x(part, 3), shift_x(part, 2), shift_x(part, 1), part])
    theirs = swap(parts)
    both = jnp.stack([jnp.where(c == 0, parts, theirs), jnp.where(c == 0, theirs, parts)])
    both = both.reshape(2, 4, 512)[:, :, :480].reshape(2, 4, 5, 4, 2, USED)
    by_row = 0.0
    for core in range(2):
        for hi in range(4):
            at = (43 * (2 * hi + core)) // 4
            by_row = by_row + jnp.pad(both[core, :, :, hi], ((0, 0), (0, 0), (0, 0), (at, 88 - USED - at)))
    by_row = by_row[..., :GROUP_ROWS].transpose(1, 2, 0, 3).reshape(-1)
    start = jnp.where(yh == 2, 3, jnp.where(yh == 3, 7, 0)) * 688
    gain_grad = lax.dynamic_slice(jnp.pad(by_row, (2816, 0)), (PIECE * j - start,), (PIECE,))

    row_gain = lax.dynamic_slice(jnp.pad(gains.reshape(-1), (0, 80)), (GROUP_ROWS * inner + first_row,), (USED,))
    weight_grad = (sums[:USED] * row_gain[:, None]).reshape(-1)
    weight_grad = lax.dynamic_slice(weight_grad, (lane,), (PIECE,))
    param_grad = weight_grad + jnp.where(inner == 95, gain_grad, 0.0)
    return (key_rows, input_grad, param_grad.reshape(1, PIECE))


def solution(mesh):
    fine = Mesh(mesh.devices.reshape(SIZES), AXES)
    tokens = P(AXES, None)
    params = P(("z", "yl", "x"), ("yh", "c"))
    return jax.shard_map(
        local, mesh=fine, in_specs=(tokens, tokens, params), out_specs=(tokens, tokens, params), check_vma=False
    )
```

```python
import jax
import jax.numpy as jnp
from jax import lax
from jax.experimental import pallas as pl
from jax.experimental.pallas import tpu as pltpu
from jax.sharding import Mesh, PartitionSpec as P

AXES = ("yh", "c", "z", "yl", "x")
SIZES = (4, 2, 12, 2, 4)
ZY = ("z", "yh", "yl")
N_ZY = 96

LANES = 128
BLK = 16
USED = 12
GROUP_ROWS = 86
PIECE = 1376
EPS = 1e-05
ROWS_PAD = 8272
STEP = 1024


def swap(a):
    return lax.ppermute(a, "c", [(0, 1), (1, 0)])


def shift_x(a, k):
    return lax.ppermute(a, "x", [(i, (i + k) % 4) for i in range(4)])


def first_row(yh, core):
    return lax.div(43 * (2 * yh + core), 4)


def sums_kernel(pos_ref, hidden_ref, cot_ref, own_ref, send_ref, inv_ref, u_ref):
    width = hidden_ref.shape[1]
    x, c = pos_ref[0], pos_ref[1]

    def squares(m, acc):
        part = hidden_ref[:, pl.ds(pl.multiple_of(m * STEP, STEP), STEP)].astype(jnp.float32)
        part = part * part
        for k in range(STEP // LANES):
            acc = acc + part[:, k * LANES : (k + 1) * LANES]
        return acc

    acc = lax.fori_loop(0, width // STEP, squares, jnp.zeros((hidden_ref.shape[0], LANES), jnp.float32))
    inv = lax.rsqrt(jnp.sum(acc, axis=1, keepdims=True) / width + EPS)
    inv_ref[...] = jnp.broadcast_to(inv, inv_ref.shape)
    cots = (cot_ref[...].astype(jnp.float32) * inv).astype(jnp.bfloat16)

    def outer(m, _):
        at = pl.multiple_of(m * STEP, STEP)
        u_ref[pl.ds(at, STEP), :] = lax.dot_general(
            hidden_ref[:, pl.ds(at, STEP)], cots, (((0,), (0,)), ((), ())), preferred_element_type=jnp.float32
        )
        return 0

    lax.fori_loop(0, width // STEP, outer, 0, unroll=2)
    u_ref[width:, :] = jnp.zeros((ROWS_PAD - width, LANES), jnp.float32)

    starts = [[GROUP_ROWS * lax.rem(x + k, 4) + first_row(yh, core) for yh in range(4)] for core in (c, 1 - c) for k in range(4)]

    def pack(q, _):
        place = (q // 2) * 8 + lax.rem(q, 2)
        base = 4 * GROUP_ROWS * q
        for side, out in enumerate((own_ref, send_ref)):
            for k in range(4):
                for yh in range(4):
                    row = base + starts[4 * side + k][yh]
                    out[k, place + 2 * yh] = u_ref[pl.ds(row, BLK), :].astype(jnp.bfloat16)
        return 0

    lax.fori_loop(0, 24, pack, 0)


def rows_kernel(pos_ref, hidden_ref, cot_ref, inv_ref, *refs):
    key_ref, grad_ref, gain_ref, s_ref, w_ref = refs[6:]
    pieces = (refs[:4], [refs[4]] + [refs[5].at[k] for k in range(3)])
    width = hidden_ref.shape[1]
    x, c = pos_ref[0], pos_ref[1]

    s_ref[1, 0:BLK, :] = jnp.zeros((BLK, LANES), jnp.float32)
    tail = jnp.zeros((22 - BLK, LANES), jnp.float32)
    one = jnp.zeros((1, LANES), jnp.float32)

    offsets = [[first_row(yh, core) for yh in range(4)] for core in (c, 1 - c)]
    bases = [GROUP_ROWS * lax.rem(x + 4 - k, 4) for k in range(4)]

    def assemble(q, _):
        place = (q // 2) * 8 + lax.rem(q, 2)
        for k in range(4):
            base = 4 * GROUP_ROWS * q + bases[k]
            for side, core in enumerate((c, 1 - c)):
                s_ref[core, pl.ds(base + 85, 1), :] = one
                for yh in range(4):
                    row = base + offsets[side][yh]
                    s_ref[core, pl.ds(row, BLK), :] = pieces[side][k][place + 2 * yh].astype(jnp.float32)
                    rest = 6 if yh < 3 else 5
                    s_ref[core, pl.ds(row + BLK, rest), :] = tail[:rest]
        return 0

    lax.fori_loop(0, 24, assemble, 0)
    gain_ref[...] = s_ref[0, width : width + 64, :] + s_ref[1, width : width + 64, :]
    inv = inv_ref[...]

    def forward(m, key):
        at = pl.multiple_of(m * STEP, STEP)
        weight = (s_ref[0, pl.ds(at, STEP), :] + s_ref[1, pl.ds(at, STEP), :]).astype(jnp.bfloat16)
        w_ref[pl.ds(at, STEP), :] = weight
        rows = []
        for k in range(STEP // LANES):
            part = hidden_ref[:, pl.ds(pl.multiple_of(at + k * LANES, LANES), LANES)].astype(jnp.float32)
            gain = gain_ref[pl.ds(m * (STEP // LANES) + k, 1), :]
            rows.append((part * inv * gain).astype(jnp.bfloat16))
        return key + jnp.dot(jnp.concatenate(rows, axis=1), weight, preferred_element_type=jnp.float32)

    key = lax.fori_loop(
        0, width // STEP, forward, jnp.zeros(key_ref.shape, jnp.float32), unroll=2
    )
    key_ref[...] = key.astype(jnp.bfloat16)
    cot = cot_ref[...]
    scale = inv * (jnp.sum(cot.astype(jnp.float32) * key, axis=1, keepdims=True) / width)

    def backward(m, _):
        at = pl.multiple_of(m * STEP, STEP)
        back = lax.dot_general(
            cot, w_ref[pl.ds(at, STEP), :], (((1,), (1,)), ((), ())), preferred_element_type=jnp.float32
        )
        for k in range(STEP // LANES):
            lanes = pl.ds(pl.multiple_of(at + k * LANES, LANES), LANES)
            part = hidden_ref[:, lanes].astype(jnp.float32)
            gain = gain_ref[pl.ds(m * (STEP // LANES) + k, 1), :]
            grad = inv * (back[:, k * LANES : (k + 1) * LANES] * gain - part * scale)
            grad_ref[:, lanes] = grad.astype(jnp.bfloat16)
        return 0

    lax.fori_loop(0, width // STEP, backward, 0, unroll=2)


def local(hidden_in, cotangent, params):
    tokens, width = hidden_in.shape
    x, c, z = lax.axis_index("x"), lax.axis_index("c"), lax.axis_index("z")
    yh, yl = lax.axis_index("yh"), lax.axis_index("yl")
    inner, j = (z * 2 + yl) * 4 + x, yh * 2 + c
    row0, lane = first_row(yh, c), (96 * j) % LANES
    pos = jnp.stack([x, c]).astype(jnp.int32)
    smem = pl.BlockSpec(memory_space=pltpu.SMEM)
    vmem = pl.BlockSpec(memory_space=pltpu.VMEM)
    bf16, f32 = jnp.bfloat16, jnp.float32

    flat = jnp.pad(params.reshape(-1), (LANES, BLK * LANES - PIECE))
    block = lax.dynamic_slice(flat, (LANES - lane,), (BLK * LANES,)).reshape(1, BLK, LANES)
    mine = lax.all_to_all(jnp.broadcast_to(block, (N_ZY, BLK, LANES)), ZY, 0, 0, tiled=True)

    half = jax.ShapeDtypeStruct((4, N_ZY, BLK, LANES), bf16)
    own, send, inv = pl.pallas_call(
        sums_kernel,
        out_shape=(half, half, jax.ShapeDtypeStruct((tokens, LANES), f32)),
        in_specs=[smem, vmem, vmem],
        out_specs=(vmem, vmem, vmem),
        scratch_shapes=[pltpu.VMEM((ROWS_PAD, LANES), f32)],
        compiler_params=pltpu.CompilerParams(vmem_limit_bytes=24 << 20),
        cost_estimate=pl.CostEstimate(flops=4 * tokens * width * LANES, bytes_accessed=8 << 20, transcendentals=0),
    )(pos, hidden_in, cotangent)
    send, mine = lax.optimization_barrier((send, mine))
    got = swap(send)
    pair = [own[k].astype(f32) + got[k].astype(f32) for k in range(4)]
    moved = [shift_x(pair[k].astype(bf16), k) for k in range(1, 4)]

    held = [mine] + [shift_x(mine, k) for k in range(1, 4)]
    other = [swap(mine), swap(jnp.stack(held[1:]))]

    total = pair[0] + moved[0].astype(f32) + moved[1].astype(f32) + moved[2].astype(f32)
    gain_part = jnp.sum(mine.astype(f32) * total, axis=-1)[:, :USED].reshape(12, 8 * USED)
    pays = [jnp.zeros((512,), f32)]
    for start in (0, 3, 7):
        pays.append(jnp.pad(gain_part[start : start + 5].reshape(-1), (0, 32)))
    pay = jnp.stack(pays).reshape(4, 1, 4, LANES)
    pay = jnp.concatenate([jnp.zeros_like(pay), pay], axis=1).reshape(8, 4, LANES)
    pay = jnp.pad(pay, ((N_ZY - 8, 0), (USED, 0), (0, 0)))
    spare = lax.broadcasted_iota(jnp.int32, (1, BLK, 1), 1) >= USED
    chunk = jnp.where(spare, pay, total).astype(bf16)
    sums = lax.all_to_all(chunk, ZY, 0, 0, tiled=True).astype(f32).sum(axis=0)

    key_rows, input_grad, gains = pl.pallas_call(
        rows_kernel,
        out_shape=(
            jax.ShapeDtypeStruct((tokens, LANES), bf16),
            jax.ShapeDtypeStruct((tokens, width), bf16),
            jax.ShapeDtypeStruct((64, LANES), f32),
        ),
        in_specs=[smem] + [vmem] * 9,
        out_specs=(vmem, vmem, vmem),
        scratch_shapes=[pltpu.VMEM((2, ROWS_PAD, LANES), f32), pltpu.VMEM((width, LANES), bf16)],
        compiler_params=pltpu.CompilerParams(vmem_limit_bytes=36 << 20),
        cost_estimate=pl.CostEstimate(flops=4 * tokens * width * LANES, bytes_accessed=10 << 20, transcendentals=0),
    )(pos, hidden_in, cotangent, inv, *held, *other)

    part = sums[USED:]
    parts = lax.all_to_all(jnp.broadcast_to(part, (8, 4, LANES)), ("c", "x"), 0, 0, tiled=True)
    both = parts.reshape(2, 4, 512)[:, :, :480].reshape(2, 4, 5, 4, 2, USED)
    by_row = 0.0
    for core in range(2):
        for hi in range(4):
            at = (43 * (2 * hi + core)) // 4
            by_row = by_row + jnp.pad(both[core, :, :, hi], ((0, 0), (0, 0), (0, 0), (at, 88 - USED - at)))
    by_row = by_row[..., :GROUP_ROWS].transpose(1, 2, 0, 3).reshape(-1)
    start = jnp.where(yh == 2, 3, jnp.where(yh == 3, 7, 0)) * 688
    gain_grad = lax.dynamic_slice(jnp.pad(by_row, (2816, 0)), (PIECE * j - start,), (PIECE,))

    row_gain = lax.dynamic_slice(jnp.pad(gains.reshape(-1), (0, 80)), (GROUP_ROWS * inner + row0,), (USED,))
    weight_grad = (sums[:USED] * row_gain[:, None]).reshape(-1)
    weight_grad = lax.dynamic_slice(weight_grad, (lane,), (PIECE,))
    param_grad = weight_grad + jnp.where(inner == 95, gain_grad, 0.0)
    return (key_rows, input_grad, param_grad.reshape(1, PIECE))


def solution(mesh):
    fine = Mesh(mesh.devices.reshape(SIZES), AXES)
    tokens = P(AXES, None)
    params = P(("z", "yl", "x"), ("yh", "c"))
    return jax.shard_map(
        local, mesh=fine, in_specs=(tokens, tokens, params), out_specs=(tokens, tokens, params), check_vma=False
    )
```

```python
import jax
import jax.numpy as jnp
from jax import lax
from jax.experimental import pallas as pl
from jax.experimental.pallas import tpu as pltpu
from jax.sharding import Mesh, PartitionSpec as P

AXES = ("yh", "c", "z", "yl", "x")
SIZES = (4, 2, 12, 2, 4)
ZY = ("z", "yh", "yl")
N_ZY = 96

LANES = 128
BLK = 16
USED = 12
GROUP_ROWS = 86
PIECE = 1376
EPS = 1e-05
ROWS_PAD = 8272
STEP = 1024


def swap(a):
    return lax.ppermute(a, "c", [(0, 1), (1, 0)])


def shift_x(a, k):
    return lax.ppermute(a, "x", [(i, (i + k) % 4) for i in range(4)])


def first_row(yh, core):
    return lax.div(43 * (2 * yh + core), 4)


def sums_kernel(pos_ref, hidden_ref, cot_ref, own_ref, send_ref, inv_ref, u_ref):
    width = hidden_ref.shape[1]
    x, c = pos_ref[0], pos_ref[1]

    def squares(m, acc):
        part = hidden_ref[:, pl.ds(pl.multiple_of(m * STEP, STEP), STEP)].astype(jnp.float32)
        part = part * part
        for k in range(STEP // LANES):
            acc = acc + part[:, k * LANES : (k + 1) * LANES]
        return acc

    acc = lax.fori_loop(0, width // STEP, squares, jnp.zeros((hidden_ref.shape[0], LANES), jnp.float32))
    inv = lax.rsqrt(jnp.sum(acc, axis=1, keepdims=True) / width + EPS)
    inv_ref[...] = jnp.broadcast_to(inv, inv_ref.shape)
    cots = (cot_ref[...].astype(jnp.float32) * inv).astype(jnp.bfloat16)

    def outer(m, _):
        at = pl.multiple_of(m * STEP, STEP)
        u_ref[pl.ds(at, STEP), :] = lax.dot_general(
            hidden_ref[:, pl.ds(at, STEP)], cots, (((0,), (0,)), ((), ())), preferred_element_type=jnp.float32
        )
        return 0

    lax.fori_loop(0, width // STEP, outer, 0, unroll=2)
    u_ref[width:, :] = jnp.zeros((ROWS_PAD - width, LANES), jnp.float32)

    starts = [[GROUP_ROWS * lax.rem(x + k, 4) + first_row(yh, core) for yh in range(4)] for core in (c, 1 - c) for k in range(4)]

    def pack(q, _):
        place = (q // 2) * 8 + lax.rem(q, 2)
        base = 4 * GROUP_ROWS * q
        for side, out in enumerate((own_ref, send_ref)):
            for k in range(4):
                for yh in range(4):
                    row = base + starts[4 * side + k][yh]
                    out[k, place + 2 * yh] = u_ref[pl.ds(row, BLK), :].astype(jnp.bfloat16)
        return 0

    lax.fori_loop(0, 24, pack, 0)


def rows_kernel(pos_ref, hidden_ref, cot_ref, inv_ref, *refs):
    key_ref, grad_ref, gain_ref, s_ref, w_ref = refs[6:]
    pieces = (refs[:4], [refs[4]] + [refs[5].at[k] for k in range(3)])
    width = hidden_ref.shape[1]
    x, c = pos_ref[0], pos_ref[1]

    s_ref[1, 0:BLK, :] = jnp.zeros((BLK, LANES), jnp.float32)
    tail = jnp.zeros((22 - BLK, LANES), jnp.float32)
    one = jnp.zeros((1, LANES), jnp.float32)

    offsets = [[first_row(yh, core) for yh in range(4)] for core in (c, 1 - c)]
    bases = [GROUP_ROWS * lax.rem(x + 4 - k, 4) for k in range(4)]

    def assemble(q, _):
        place = (q // 2) * 8 + lax.rem(q, 2)
        for k in range(4):
            base = 4 * GROUP_ROWS * q + bases[k]
            for side, core in enumerate((c, 1 - c)):
                s_ref[core, pl.ds(base + 85, 1), :] = one
                for yh in range(4):
                    row = base + offsets[side][yh]
                    s_ref[core, pl.ds(row, BLK), :] = pieces[side][k][place + 2 * yh].astype(jnp.float32)
                    rest = 6 if yh < 3 else 5
                    s_ref[core, pl.ds(row + BLK, rest), :] = tail[:rest]
        return 0

    lax.fori_loop(0, 24, assemble, 0)
    gain_ref[...] = s_ref[0, width : width + 64, :] + s_ref[1, width : width + 64, :]
    inv = inv_ref[...]

    def forward(m, key):
        at = pl.multiple_of(m * STEP, STEP)
        weight = (s_ref[0, pl.ds(at, STEP), :] + s_ref[1, pl.ds(at, STEP), :]).astype(jnp.bfloat16)
        w_ref[pl.ds(at, STEP), :] = weight
        rows = []
        for k in range(STEP // LANES):
            part = hidden_ref[:, pl.ds(pl.multiple_of(at + k * LANES, LANES), LANES)].astype(jnp.float32)
            gain = gain_ref[pl.ds(m * (STEP // LANES) + k, 1), :]
            rows.append((part * inv * gain).astype(jnp.bfloat16))
        return key + jnp.dot(jnp.concatenate(rows, axis=1), weight, preferred_element_type=jnp.float32)

    key = lax.fori_loop(
        0, width // STEP, forward, jnp.zeros(key_ref.shape, jnp.float32), unroll=2
    )
    key_ref[...] = key.astype(jnp.bfloat16)
    cot = cot_ref[...]
    scale = inv * (jnp.sum(cot.astype(jnp.float32) * key, axis=1, keepdims=True) / width)

    def backward(m, _):
        at = pl.multiple_of(m * STEP, STEP)
        back = lax.dot_general(
            cot, w_ref[pl.ds(at, STEP), :], (((1,), (1,)), ((), ())), preferred_element_type=jnp.float32
        )
        for k in range(STEP // LANES):
            lanes = pl.ds(pl.multiple_of(at + k * LANES, LANES), LANES)
            part = hidden_ref[:, lanes].astype(jnp.float32)
            gain = gain_ref[pl.ds(m * (STEP // LANES) + k, 1), :]
            grad = inv * (back[:, k * LANES : (k + 1) * LANES] * gain - part * scale)
            grad_ref[:, lanes] = grad.astype(jnp.bfloat16)
        return 0

    lax.fori_loop(0, width // STEP, backward, 0, unroll=2)


def local(hidden_in, cotangent, params):
    tokens, width = hidden_in.shape
    x, c, z = lax.axis_index("x"), lax.axis_index("c"), lax.axis_index("z")
    yh, yl = lax.axis_index("yh"), lax.axis_index("yl")
    inner, j = (z * 2 + yl) * 4 + x, yh * 2 + c
    row0, lane = first_row(yh, c), (96 * j) % LANES
    pos = jnp.stack([x, c]).astype(jnp.int32)
    smem = pl.BlockSpec(memory_space=pltpu.SMEM)
    vmem = pl.BlockSpec(memory_space=pltpu.VMEM)
    bf16, f32 = jnp.bfloat16, jnp.float32

    flat = jnp.pad(params.reshape(-1), (LANES, BLK * LANES - PIECE))
    block = lax.dynamic_slice(flat, (LANES - lane,), (BLK * LANES,)).reshape(1, BLK, LANES)
    mine = lax.all_to_all(jnp.broadcast_to(block, (N_ZY, BLK, LANES)), ZY, 0, 0, tiled=True)

    half = jax.ShapeDtypeStruct((4, N_ZY, BLK, LANES), bf16)
    own, send, inv = pl.pallas_call(
        sums_kernel,
        out_shape=(half, half, jax.ShapeDtypeStruct((tokens, LANES), f32)),
        in_specs=[smem, vmem, vmem],
        out_specs=(vmem, vmem, vmem),
        scratch_shapes=[pltpu.VMEM((ROWS_PAD, LANES), f32)],
        compiler_params=pltpu.CompilerParams(vmem_limit_bytes=24 << 20),
        cost_estimate=pl.CostEstimate(flops=4 * tokens * width * LANES, bytes_accessed=8 << 20, transcendentals=0),
    )(pos, hidden_in, cotangent)
    got = swap(send)
    pair = [own[k].astype(f32) + got[k].astype(f32) for k in range(4)]
    moved = [shift_x(pair[k].astype(bf16), k) for k in range(1, 4)]
    moved, mine = lax.optimization_barrier((moved, mine))

    held = [mine] + [shift_x(mine, k) for k in range(1, 4)]
    other = [swap(mine), swap(jnp.stack(held[1:]))]

    total = pair[0] + moved[0].astype(f32) + moved[1].astype(f32) + moved[2].astype(f32)
    gain_part = jnp.sum(mine.astype(f32) * total, axis=-1)[:, :USED].reshape(12, 8 * USED)
    pays = [jnp.zeros((512,), f32)]
    for start in (0, 3, 7):
        pays.append(jnp.pad(gain_part[start : start + 5].reshape(-1), (0, 32)))
    pay = jnp.stack(pays).reshape(4, 1, 4, LANES)
    pay = jnp.concatenate([jnp.zeros_like(pay), pay], axis=1).reshape(8, 4, LANES)
    pay = jnp.pad(pay, ((N_ZY - 8, 0), (USED, 0), (0, 0)))
    spare = lax.broadcasted_iota(jnp.int32, (1, BLK, 1), 1) >= USED
    chunk = jnp.where(spare, pay, total).astype(bf16)
    sums = lax.all_to_all(chunk, ZY, 0, 0, tiled=True).astype(f32).sum(axis=0)

    key_rows, input_grad, gains = pl.pallas_call(
        rows_kernel,
        out_shape=(
            jax.ShapeDtypeStruct((tokens, LANES), bf16),
            jax.ShapeDtypeStruct((tokens, width), bf16),
            jax.ShapeDtypeStruct((64, LANES), f32),
        ),
        in_specs=[smem] + [vmem] * 9,
        out_specs=(vmem, vmem, vmem),
        scratch_shapes=[pltpu.VMEM((2, ROWS_PAD, LANES), f32), pltpu.VMEM((width, LANES), bf16)],
        compiler_params=pltpu.CompilerParams(vmem_limit_bytes=36 << 20),
        cost_estimate=pl.CostEstimate(flops=4 * tokens * width * LANES, bytes_accessed=10 << 20, transcendentals=0),
    )(pos, hidden_in, cotangent, inv, *held, *other)

    part, gains = lax.optimization_barrier((sums[USED:], gains))
    parts = lax.all_to_all(jnp.broadcast_to(part, (8, 4, LANES)), ("c", "x"), 0, 0, tiled=True)
    both = parts.reshape(2, 4, 512)[:, :, :480].reshape(2, 4, 5, 4, 2, USED)
    by_row = 0.0
    for core in range(2):
        for hi in range(4):
            at = (43 * (2 * hi + core)) // 4
            by_row = by_row + jnp.pad(both[core, :, :, hi], ((0, 0), (0, 0), (0, 0), (at, 88 - USED - at)))
    by_row = by_row[..., :GROUP_ROWS].transpose(1, 2, 0, 3).reshape(-1)
    start = jnp.where(yh == 2, 3, jnp.where(yh == 3, 7, 0)) * 688
    gain_grad = lax.dynamic_slice(jnp.pad(by_row, (2816, 0)), (PIECE * j - start,), (PIECE,))

    row_gain = lax.dynamic_slice(jnp.pad(gains.reshape(-1), (0, 80)), (GROUP_ROWS * inner + row0,), (USED,))
    weight_grad = (sums[:USED] * row_gain[:, None]).reshape(-1)
    weight_grad = lax.dynamic_slice(weight_grad, (lane,), (PIECE,))
    param_grad = weight_grad + jnp.where(inner == 95, gain_grad, 0.0)
    return (key_rows, input_grad, param_grad.reshape(1, PIECE))


def solution(mesh):
    fine = Mesh(mesh.devices.reshape(SIZES), AXES)
    tokens = P(AXES, None)
    params = P(("z", "yl", "x"), ("yh", "c"))
    return jax.shard_map(
        local, mesh=fine, in_specs=(tokens, tokens, params), out_specs=(tokens, tokens, params), check_vma=False
    )
```

```python
import jax
import jax.numpy as jnp
from jax import lax
from jax.experimental import pallas as pl
from jax.experimental.pallas import tpu as pltpu
from jax.sharding import Mesh, PartitionSpec as P

AXES = ("yh", "c", "z", "yl", "x")
SIZES = (4, 2, 12, 2, 4)
ZY = ("z", "yh", "yl")
N_ZY = 96

LANES = 128
BLK = 16
USED = 12
GROUP_ROWS = 86
PIECE = 1376
EPS = 1e-05
ROWS_PAD = 8272
STEP = 1024


def swap(a):
    return lax.ppermute(a, "c", [(0, 1), (1, 0)])


def shift_x(a, k):
    return lax.ppermute(a, "x", [(i, (i + k) % 4) for i in range(4)])


def first_row(yh, core):
    return lax.div(43 * (2 * yh + core), 4)


def sums_kernel(pos_ref, hidden_ref, cot_ref, own_ref, send_ref, inv_ref, u_ref):
    width = hidden_ref.shape[1]
    x, c = pos_ref[0], pos_ref[1]

    def squares(m, acc):
        part = hidden_ref[:, pl.ds(pl.multiple_of(m * STEP, STEP), STEP)].astype(jnp.float32)
        part = part * part
        for k in range(STEP // LANES):
            acc = acc + part[:, k * LANES : (k + 1) * LANES]
        return acc

    acc = lax.fori_loop(0, width // STEP, squares, jnp.zeros((hidden_ref.shape[0], LANES), jnp.float32))
    inv = lax.rsqrt(jnp.sum(acc, axis=1, keepdims=True) / width + EPS)
    inv_ref[...] = jnp.broadcast_to(inv, inv_ref.shape)
    cots = (cot_ref[...].astype(jnp.float32) * inv).astype(jnp.bfloat16)

    def outer(m, _):
        at = pl.multiple_of(m * STEP, STEP)
        u_ref[pl.ds(at, STEP), :] = lax.dot_general(
            hidden_ref[:, pl.ds(at, STEP)], cots, (((0,), (0,)), ((), ())), preferred_element_type=jnp.float32
        )
        return 0

    lax.fori_loop(0, width // STEP, outer, 0, unroll=2)
    u_ref[width:, :] = jnp.zeros((ROWS_PAD - width, LANES), jnp.float32)

    starts = [[GROUP_ROWS * lax.rem(x + k, 4) + first_row(yh, core) for yh in range(4)] for core in (c, 1 - c) for k in range(4)]

    def pack(q, _):
        place = (q // 2) * 8 + lax.rem(q, 2)
        base = 4 * GROUP_ROWS * q
        for side, out in enumerate((own_ref, send_ref)):
            for k in range(4):
                for yh in range(4):
                    row = base + starts[4 * side + k][yh]
                    out[k, place + 2 * yh] = u_ref[pl.ds(row, BLK), :].astype(jnp.bfloat16)
        return 0

    lax.fori_loop(0, 24, pack, 0)


def rows_kernel(pos_ref, hidden_ref, cot_ref, inv_ref, *refs):
    key_ref, grad_ref, gain_ref, s_ref, w_ref = refs[6:]
    pieces = (refs[:4], [refs[4]] + [refs[5].at[k] for k in range(3)])
    width = hidden_ref.shape[1]
    x, c = pos_ref[0], pos_ref[1]

    s_ref[1, 0:BLK, :] = jnp.zeros((BLK, LANES), jnp.float32)
    tail = jnp.zeros((22 - BLK, LANES), jnp.float32)
    one = jnp.zeros((1, LANES), jnp.float32)

    offsets = [[first_row(yh, core) for yh in range(4)] for core in (c, 1 - c)]
    bases = [GROUP_ROWS * lax.rem(x + 4 - k, 4) for k in range(4)]

    def assemble(q, _):
        place = (q // 2) * 8 + lax.rem(q, 2)
        for k in range(4):
            base = 4 * GROUP_ROWS * q + bases[k]
            for side, core in enumerate((c, 1 - c)):
                s_ref[core, pl.ds(base + 85, 1), :] = one
                for yh in range(4):
                    row = base + offsets[side][yh]
                    s_ref[core, pl.ds(row, BLK), :] = pieces[side][k][place + 2 * yh].astype(jnp.float32)
                    rest = 6 if yh < 3 else 5
                    s_ref[core, pl.ds(row + BLK, rest), :] = tail[:rest]
        return 0

    lax.fori_loop(0, 24, assemble, 0)
    gain_ref[...] = s_ref[0, width : width + 64, :] + s_ref[1, width : width + 64, :]
    inv = inv_ref[...]

    def forward(m, key):
        at = pl.multiple_of(m * STEP, STEP)
        weight = (s_ref[0, pl.ds(at, STEP), :] + s_ref[1, pl.ds(at, STEP), :]).astype(jnp.bfloat16)
        w_ref[pl.ds(at, STEP), :] = weight
        rows = []
        for k in range(STEP // LANES):
            part = hidden_ref[:, pl.ds(pl.multiple_of(at + k * LANES, LANES), LANES)].astype(jnp.float32)
            gain = gain_ref[pl.ds(m * (STEP // LANES) + k, 1), :]
            rows.append((part * inv * gain).astype(jnp.bfloat16))
        return key + jnp.dot(jnp.concatenate(rows, axis=1), weight, preferred_element_type=jnp.float32)

    key = lax.fori_loop(
        0, width // STEP, forward, jnp.zeros(key_ref.shape, jnp.float32), unroll=2
    )
    key_ref[...] = key.astype(jnp.bfloat16)
    cot = cot_ref[...]
    scale = inv * (jnp.sum(cot.astype(jnp.float32) * key, axis=1, keepdims=True) / width)

    def backward(m, _):
        at = pl.multiple_of(m * STEP, STEP)
        back = lax.dot_general(
            cot, w_ref[pl.ds(at, STEP), :], (((1,), (1,)), ((), ())), preferred_element_type=jnp.float32
        )
        for k in range(STEP // LANES):
            lanes = pl.ds(pl.multiple_of(at + k * LANES, LANES), LANES)
            part = hidden_ref[:, lanes].astype(jnp.float32)
            gain = gain_ref[pl.ds(m * (STEP // LANES) + k, 1), :]
            grad = inv * (back[:, k * LANES : (k + 1) * LANES] * gain - part * scale)
            grad_ref[:, lanes] = grad.astype(jnp.bfloat16)
        return 0

    lax.fori_loop(0, width // STEP, backward, 0, unroll=2)


def local(hidden_in, cotangent, params):
    tokens, width = hidden_in.shape
    x, c, z = lax.axis_index("x"), lax.axis_index("c"), lax.axis_index("z")
    yh, yl = lax.axis_index("yh"), lax.axis_index("yl")
    inner, j = (z * 2 + yl) * 4 + x, yh * 2 + c
    row0, lane = first_row(yh, c), (96 * j) % LANES
    pos = jnp.stack([x, c]).astype(jnp.int32)
    smem = pl.BlockSpec(memory_space=pltpu.SMEM)
    vmem = pl.BlockSpec(memory_space=pltpu.VMEM)
    bf16, f32 = jnp.bfloat16, jnp.float32

    flat = jnp.pad(params.reshape(-1), (LANES, BLK * LANES - PIECE))
    block = lax.dynamic_slice(flat, (LANES - lane,), (BLK * LANES,)).reshape(1, BLK, LANES)
    mine = lax.all_to_all(jnp.broadcast_to(block, (N_ZY, BLK, LANES)), ZY, 0, 0, tiled=True)

    half = jax.ShapeDtypeStruct((4, N_ZY, BLK, LANES), bf16)
    own, send, inv = pl.pallas_call(
        sums_kernel,
        out_shape=(half, half, jax.ShapeDtypeStruct((tokens, LANES), f32)),
        in_specs=[smem, vmem, vmem],
        out_specs=(vmem, vmem, vmem),
        scratch_shapes=[pltpu.VMEM((ROWS_PAD, LANES), f32)],
        compiler_params=pltpu.CompilerParams(vmem_limit_bytes=24 << 20),
        cost_estimate=pl.CostEstimate(flops=4 * tokens * width * LANES, bytes_accessed=8 << 20, transcendentals=0),
    )(pos, hidden_in, cotangent)
    got = swap(send)
    pair = [own[k].astype(f32) + got[k].astype(f32) for k in range(4)]
    moved = [shift_x(pair[k].astype(bf16), k) for k in range(1, 4)]

    total = pair[0] + moved[0].astype(f32) + moved[1].astype(f32) + moved[2].astype(f32)
    gain_part = jnp.sum(mine.astype(f32) * total, axis=-1)[:, :USED].reshape(12, 8 * USED)
    pays = [jnp.zeros((512,), f32)]
    for start in (0, 3, 7):
        pays.append(jnp.pad(gain_part[start : start + 5].reshape(-1), (0, 32)))
    pay = jnp.stack(pays).reshape(4, 1, 4, LANES)
    pay = jnp.concatenate([jnp.zeros_like(pay), pay], axis=1).reshape(8, 4, LANES)
    pay = jnp.pad(pay, ((N_ZY - 8, 0), (USED, 0), (0, 0)))
    spare = lax.broadcasted_iota(jnp.int32, (1, BLK, 1), 1) >= USED
    chunk, mine = lax.optimization_barrier((jnp.where(spare, pay, total).astype(bf16), mine))

    held = [mine] + [shift_x(mine, k) for k in range(1, 4)]
    other = [swap(mine), swap(jnp.stack(held[1:]))]
    received = lax.all_to_all(chunk, ZY, 0, 0, tiled=True)

    key_rows, input_grad, gains = pl.pallas_call(
        rows_kernel,
        out_shape=(
            jax.ShapeDtypeStruct((tokens, LANES), bf16),
            jax.ShapeDtypeStruct((tokens, width), bf16),
            jax.ShapeDtypeStruct((64, LANES), f32),
        ),
        in_specs=[smem] + [vmem] * 9,
        out_specs=(vmem, vmem, vmem),
        scratch_shapes=[pltpu.VMEM((2, ROWS_PAD, LANES), f32), pltpu.VMEM((width, LANES), bf16)],
        compiler_params=pltpu.CompilerParams(vmem_limit_bytes=36 << 20),
        cost_estimate=pl.CostEstimate(flops=4 * tokens * width * LANES, bytes_accessed=10 << 20, transcendentals=0),
    )(pos, hidden_in, cotangent, inv, *held, *other)

    received, gains = lax.optimization_barrier((received, gains))
    sums = received.astype(f32).sum(axis=0)
    part = sums[USED:]
    parts = lax.all_to_all(jnp.broadcast_to(part, (8, 4, LANES)), ("c", "x"), 0, 0, tiled=True)
    both = parts.reshape(2, 4, 512)[:, :, :480].reshape(2, 4, 5, 4, 2, USED)
    by_row = 0.0
    for core in range(2):
        for hi in range(4):
            at = (43 * (2 * hi + core)) // 4
            by_row = by_row + jnp.pad(both[core, :, :, hi], ((0, 0), (0, 0), (0, 0), (at, 88 - USED - at)))
    by_row = by_row[..., :GROUP_ROWS].transpose(1, 2, 0, 3).reshape(-1)
    start = jnp.where(yh == 2, 3, jnp.where(yh == 3, 7, 0)) * 688
    gain_grad = lax.dynamic_slice(jnp.pad(by_row, (2816, 0)), (PIECE * j - start,), (PIECE,))

    row_gain = lax.dynamic_slice(jnp.pad(gains.reshape(-1), (0, 80)), (GROUP_ROWS * inner + row0,), (USED,))
    weight_grad = (sums[:USED] * row_gain[:, None]).reshape(-1)
    weight_grad = lax.dynamic_slice(weight_grad, (lane,), (PIECE,))
    param_grad = weight_grad + jnp.where(inner == 95, gain_grad, 0.0)
    return (key_rows, input_grad, param_grad.reshape(1, PIECE))


def solution(mesh):
    fine = Mesh(mesh.devices.reshape(SIZES), AXES)
    tokens = P(AXES, None)
    params = P(("z", "yl", "x"), ("yh", "c"))
    return jax.shard_map(
        local, mesh=fine, in_specs=(tokens, tokens, params), out_specs=(tokens, tokens, params), check_vma=False
    )
```

```python
import jax
import jax.numpy as jnp
from jax import lax
from jax.experimental import pallas as pl
from jax.experimental.pallas import tpu as pltpu
from jax.sharding import Mesh, PartitionSpec as P

AXES = ("yh", "c", "z", "yl", "x")
SIZES = (4, 2, 12, 2, 4)
ZY = ("z", "yh", "yl")
N_ZY = 96

LANES = 128
BLK = 16
USED = 12
GROUP_ROWS = 86
PIECE = 1376
EPS = 1e-05
ROWS_PAD = 8272
STEP = 1024


def swap(a):
    return lax.ppermute(a, "c", [(0, 1), (1, 0)])


def shift_x(a, k):
    return lax.ppermute(a, "x", [(i, (i + k) % 4) for i in range(4)])


def first_row(yh, core):
    return lax.div(43 * (2 * yh + core), 4)


def sums_kernel(pos_ref, hidden_ref, cot_ref, own_ref, send_ref, inv_ref, u_ref):
    width = hidden_ref.shape[1]
    x, c = pos_ref[0], pos_ref[1]

    def squares(m, acc):
        part = hidden_ref[:, pl.ds(pl.multiple_of(m * STEP, STEP), STEP)].astype(jnp.float32)
        part = part * part
        for k in range(STEP // LANES):
            acc = acc + part[:, k * LANES : (k + 1) * LANES]
        return acc

    acc = lax.fori_loop(0, width // STEP, squares, jnp.zeros((hidden_ref.shape[0], LANES), jnp.float32))
    inv = lax.rsqrt(jnp.sum(acc, axis=1, keepdims=True) / width + EPS)
    inv_ref[...] = jnp.broadcast_to(inv, inv_ref.shape)
    cots = (cot_ref[...].astype(jnp.float32) * inv).astype(jnp.bfloat16)

    def outer(m, _):
        at = pl.multiple_of(m * STEP, STEP)
        u_ref[pl.ds(at, STEP), :] = lax.dot_general(
            hidden_ref[:, pl.ds(at, STEP)], cots, (((0,), (0,)), ((), ())), preferred_element_type=jnp.float32
        )
        return 0

    lax.fori_loop(0, width // STEP, outer, 0, unroll=2)
    u_ref[width:, :] = jnp.zeros((ROWS_PAD - width, LANES), jnp.float32)

    starts = [[GROUP_ROWS * lax.rem(x + k, 4) + first_row(yh, core) for yh in range(4)] for core in (c, 1 - c) for k in range(4)]

    def pack(q, _):
        place = (q // 2) * 8 + lax.rem(q, 2)
        base = 4 * GROUP_ROWS * q
        for side, out in enumerate((own_ref, send_ref)):
            for k in range(4):
                for yh in range(4):
                    row = base + starts[4 * side + k][yh]
                    out[k, place + 2 * yh] = u_ref[pl.ds(row, BLK), :].astype(jnp.bfloat16)
        return 0

    lax.fori_loop(0, 24, pack, 0)


def rows_kernel(pos_ref, hidden_ref, cot_ref, inv_ref, *refs):
    key_ref, grad_ref, gain_ref, s_ref, w_ref = refs[6:]
    pieces = (refs[:4], [refs[4]] + [refs[5].at[k] for k in range(3)])
    width = hidden_ref.shape[1]
    x, c = pos_ref[0], pos_ref[1]

    s_ref[1, 0:BLK, :] = jnp.zeros((BLK, LANES), jnp.float32)
    tail = jnp.zeros((22 - BLK, LANES), jnp.float32)
    one = jnp.zeros((1, LANES), jnp.float32)

    offsets = [[first_row(yh, core) for yh in range(4)] for core in (c, 1 - c)]
    bases = [GROUP_ROWS * lax.rem(x + 4 - k, 4) for k in range(4)]

    def assemble(q, _):
        place = (q // 2) * 8 + lax.rem(q, 2)
        for k in range(4):
            base = 4 * GROUP_ROWS * q + bases[k]
            for side, core in enumerate((c, 1 - c)):
                s_ref[core, pl.ds(base + 85, 1), :] = one
                for yh in range(4):
                    row = base + offsets[side][yh]
                    s_ref[core, pl.ds(row, BLK), :] = pieces[side][k][place + 2 * yh].astype(jnp.float32)
                    rest = 6 if yh < 3 else 5
                    s_ref[core, pl.ds(row + BLK, rest), :] = tail[:rest]
        return 0

    lax.fori_loop(0, 24, assemble, 0)
    gain_ref[...] = s_ref[0, width : width + 64, :] + s_ref[1, width : width + 64, :]
    inv = inv_ref[...]

    def forward(m, key):
        at = pl.multiple_of(m * STEP, STEP)
        weight = (s_ref[0, pl.ds(at, STEP), :] + s_ref[1, pl.ds(at, STEP), :]).astype(jnp.bfloat16)
        w_ref[pl.ds(at, STEP), :] = weight
        rows = []
        for k in range(STEP // LANES):
            part = hidden_ref[:, pl.ds(pl.multiple_of(at + k * LANES, LANES), LANES)].astype(jnp.float32)
            gain = gain_ref[pl.ds(m * (STEP // LANES) + k, 1), :]
            rows.append((part * inv * gain).astype(jnp.bfloat16))
        return key + jnp.dot(jnp.concatenate(rows, axis=1), weight, preferred_element_type=jnp.float32)

    key = lax.fori_loop(
        0, width // STEP, forward, jnp.zeros(key_ref.shape, jnp.float32), unroll=2
    )
    key_ref[...] = key.astype(jnp.bfloat16)
    cot = cot_ref[...]
    scale = inv * (jnp.sum(cot.astype(jnp.float32) * key, axis=1, keepdims=True) / width)

    def backward(m, _):
        at = pl.multiple_of(m * STEP, STEP)
        back = lax.dot_general(
            cot, w_ref[pl.ds(at, STEP), :], (((1,), (1,)), ((), ())), preferred_element_type=jnp.float32
        )
        for k in range(STEP // LANES):
            lanes = pl.ds(pl.multiple_of(at + k * LANES, LANES), LANES)
            part = hidden_ref[:, lanes].astype(jnp.float32)
            gain = gain_ref[pl.ds(m * (STEP // LANES) + k, 1), :]
            grad = inv * (back[:, k * LANES : (k + 1) * LANES] * gain - part * scale)
            grad_ref[:, lanes] = grad.astype(jnp.bfloat16)
        return 0

    lax.fori_loop(0, width // STEP, backward, 0, unroll=2)


def local(hidden_in, cotangent, params):
    tokens, width = hidden_in.shape
    x, c, z = lax.axis_index("x"), lax.axis_index("c"), lax.axis_index("z")
    yh, yl = lax.axis_index("yh"), lax.axis_index("yl")
    inner, j = (z * 2 + yl) * 4 + x, yh * 2 + c
    row0, lane = first_row(yh, c), (96 * j) % LANES
    pos = jnp.stack([x, c]).astype(jnp.int32)
    smem = pl.BlockSpec(memory_space=pltpu.SMEM)
    vmem = pl.BlockSpec(memory_space=pltpu.VMEM)
    bf16, f32 = jnp.bfloat16, jnp.float32

    flat = jnp.pad(params.reshape(-1), (LANES, BLK * LANES - PIECE))
    block = lax.dynamic_slice(flat, (LANES - lane,), (BLK * LANES,)).reshape(1, BLK, LANES)
    mine = lax.all_to_all(jnp.broadcast_to(block, (N_ZY, BLK, LANES)), ZY, 0, 0, tiled=True)

    half = jax.ShapeDtypeStruct((4, N_ZY, BLK, LANES), bf16)
    own, send, inv = pl.pallas_call(
        sums_kernel,
        out_shape=(half, half, jax.ShapeDtypeStruct((tokens, LANES), f32)),
        in_specs=[smem, vmem, vmem],
        out_specs=(vmem, vmem, vmem),
        scratch_shapes=[pltpu.VMEM((ROWS_PAD, LANES), f32)],
        compiler_params=pltpu.CompilerParams(vmem_limit_bytes=24 << 20),
        cost_estimate=pl.CostEstimate(flops=4 * tokens * width * LANES, bytes_accessed=8 << 20, transcendentals=0),
    )(pos, hidden_in, cotangent)
    got = swap(send)
    pair = [own[k].astype(f32) + got[k].astype(f32) for k in range(4)]
    moved = [shift_x(pair[k].astype(bf16), k) for k in range(1, 4)]
    moved[0], mine = lax.optimization_barrier((moved[0], mine))
    held = [mine] + [shift_x(mine, k) for k in range(1, 4)]
    other = [swap(mine), swap(jnp.stack(held[1:]))]


    total = pair[0] + moved[0].astype(f32) + moved[1].astype(f32) + moved[2].astype(f32)
    gain_part = jnp.sum(mine.astype(f32) * total, axis=-1)[:, :USED].reshape(12, 8 * USED)
    pays = [jnp.zeros((512,), f32)]
    for start in (0, 3, 7):
        pays.append(jnp.pad(gain_part[start : start + 5].reshape(-1), (0, 32)))
    pay = jnp.stack(pays).reshape(4, 1, 4, LANES)
    pay = jnp.concatenate([jnp.zeros_like(pay), pay], axis=1).reshape(8, 4, LANES)
    pay = jnp.pad(pay, ((N_ZY - 8, 0), (USED, 0), (0, 0)))
    spare = lax.broadcasted_iota(jnp.int32, (1, BLK, 1), 1) >= USED
    chunk = jnp.where(spare, pay, total).astype(bf16)
    received = lax.all_to_all(chunk, ZY, 0, 0, tiled=True)

    key_rows, input_grad, gains = pl.pallas_call(
        rows_kernel,
        out_shape=(
            jax.ShapeDtypeStruct((tokens, LANES), bf16),
            jax.ShapeDtypeStruct((tokens, width), bf16),
            jax.ShapeDtypeStruct((64, LANES), f32),
        ),
        in_specs=[smem] + [vmem] * 9,
        out_specs=(vmem, vmem, vmem),
        scratch_shapes=[pltpu.VMEM((2, ROWS_PAD, LANES), f32), pltpu.VMEM((width, LANES), bf16)],
        compiler_params=pltpu.CompilerParams(vmem_limit_bytes=36 << 20),
        cost_estimate=pl.CostEstimate(flops=4 * tokens * width * LANES, bytes_accessed=10 << 20, transcendentals=0),
    )(pos, hidden_in, cotangent, inv, *held, *other)

    sums = received.astype(f32).sum(axis=0)
    part = sums[USED:]
    parts = lax.all_to_all(jnp.broadcast_to(part, (8, 4, LANES)), ("c", "x"), 0, 0, tiled=True)
    parts, gains = lax.optimization_barrier((parts, gains))
    both = parts.reshape(2, 4, 512)[:, :, :480].reshape(2, 4, 5, 4, 2, USED)
    by_row = 0.0
    for core in range(2):
        for hi in range(4):
            at = (43 * (2 * hi + core)) // 4
            by_row = by_row + jnp.pad(both[core, :, :, hi], ((0, 0), (0, 0), (0, 0), (at, 88 - USED - at)))
    by_row = by_row[..., :GROUP_ROWS].transpose(1, 2, 0, 3).reshape(-1)
    start = jnp.where(yh == 2, 3, jnp.where(yh == 3, 7, 0)) * 688
    gain_grad = lax.dynamic_slice(jnp.pad(by_row, (2816, 0)), (PIECE * j - start,), (PIECE,))

    row_gain = lax.dynamic_slice(jnp.pad(gains.reshape(-1), (0, 80)), (GROUP_ROWS * inner + row0,), (USED,))
    weight_grad = (sums[:USED] * row_gain[:, None]).reshape(-1)
    weight_grad = lax.dynamic_slice(weight_grad, (lane,), (PIECE,))
    param_grad = weight_grad + jnp.where(inner == 95, gain_grad, 0.0)
    return (key_rows, input_grad, param_grad.reshape(1, PIECE))


def solution(mesh):
    fine = Mesh(mesh.devices.reshape(SIZES), AXES)
    tokens = P(AXES, None)
    params = P(("z", "yl", "x"), ("yh", "c"))
    return jax.shard_map(
        local, mesh=fine, in_specs=(tokens, tokens, params), out_specs=(tokens, tokens, params), check_vma=False
    )
```

```python
import jax
import jax.numpy as jnp
from jax import lax
from jax.experimental import pallas as pl
from jax.experimental.pallas import tpu as pltpu
from jax.sharding import Mesh, PartitionSpec as P

AXES = ("yh", "c", "z", "yl", "x")
SIZES = (4, 2, 12, 2, 4)
ZY = ("z", "yh", "yl")
N_ZY = 96

LANES = 128
BLK = 16
USED = 12
GROUP_ROWS = 86
PIECE = 1376
EPS = 1e-05
ROWS_PAD = 8272
STEP = 1024


def swap(a):
    return lax.ppermute(a, "c", [(0, 1), (1, 0)])


def shift_x(a, k):
    return lax.ppermute(a, "x", [(i, (i + k) % 4) for i in range(4)])


def first_row(yh, core):
    return lax.div(43 * (2 * yh + core), 4)


def sums_kernel(pos_ref, hidden_ref, cot_ref, own_ref, send_ref, inv_ref, u_ref):
    width = hidden_ref.shape[1]
    x, c = pos_ref[0], pos_ref[1]

    def squares(m, acc):
        part = hidden_ref[:, pl.ds(pl.multiple_of(m * STEP, STEP), STEP)].astype(jnp.float32)
        part = part * part
        for k in range(STEP // LANES):
            acc = acc + part[:, k * LANES : (k + 1) * LANES]
        return acc

    acc = lax.fori_loop(0, width // STEP, squares, jnp.zeros((hidden_ref.shape[0], LANES), jnp.float32))
    inv = lax.rsqrt(jnp.sum(acc, axis=1, keepdims=True) / width + EPS)
    inv_ref[...] = jnp.broadcast_to(inv, inv_ref.shape)
    cots = (cot_ref[...].astype(jnp.float32) * inv).astype(jnp.bfloat16)

    def outer(m, _):
        at = pl.multiple_of(m * STEP, STEP)
        u_ref[pl.ds(at, STEP), :] = lax.dot_general(
            hidden_ref[:, pl.ds(at, STEP)], cots, (((0,), (0,)), ((), ())), preferred_element_type=jnp.float32
        )
        return 0

    lax.fori_loop(0, width // STEP, outer, 0, unroll=2)
    u_ref[width:, :] = jnp.zeros((ROWS_PAD - width, LANES), jnp.float32)

    starts = [[GROUP_ROWS * lax.rem(x + k, 4) + first_row(yh, core) for yh in range(4)] for core in (c, 1 - c) for k in range(4)]

    def pack(q, _):
        place = (q // 2) * 8 + lax.rem(q, 2)
        base = 4 * GROUP_ROWS * q
        for side, out in enumerate((own_ref, send_ref)):
            for k in range(4):
                for yh in range(4):
                    row = base + starts[4 * side + k][yh]
                    out[k, place + 2 * yh] = u_ref[pl.ds(row, BLK), :].astype(jnp.bfloat16)
        return 0

    lax.fori_loop(0, 24, pack, 0)


def rows_kernel(pos_ref, hidden_ref, cot_ref, inv_ref, *refs):
    key_ref, grad_ref, gain_ref, s_ref, w_ref = refs[6:]
    pieces = (refs[:4], [refs[4]] + [refs[5].at[k] for k in range(3)])
    width = hidden_ref.shape[1]
    x, c = pos_ref[0], pos_ref[1]

    s_ref[1, 0:BLK, :] = jnp.zeros((BLK, LANES), jnp.float32)
    tail = jnp.zeros((22 - BLK, LANES), jnp.float32)
    one = jnp.zeros((1, LANES), jnp.float32)

    offsets = [[first_row(yh, core) for yh in range(4)] for core in (c, 1 - c)]
    bases = [GROUP_ROWS * lax.rem(x + 4 - k, 4) for k in range(4)]

    def assemble(q, _):
        place = (q // 2) * 8 + lax.rem(q, 2)
        for k in range(4):
            base = 4 * GROUP_ROWS * q + bases[k]
            for side, core in enumerate((c, 1 - c)):
                s_ref[core, pl.ds(base + 85, 1), :] = one
                for yh in range(4):
                    row = base + offsets[side][yh]
                    s_ref[core, pl.ds(row, BLK), :] = pieces[side][k][place + 2 * yh].astype(jnp.float32)
                    rest = 6 if yh < 3 else 5
                    s_ref[core, pl.ds(row + BLK, rest), :] = tail[:rest]
        return 0

    lax.fori_loop(0, 24, assemble, 0)
    gain_ref[...] = s_ref[0, width : width + 64, :] + s_ref[1, width : width + 64, :]
    inv = inv_ref[...]

    def forward(m, key):
        at = pl.multiple_of(m * STEP, STEP)
        weight = (s_ref[0, pl.ds(at, STEP), :] + s_ref[1, pl.ds(at, STEP), :]).astype(jnp.bfloat16)
        w_ref[pl.ds(at, STEP), :] = weight
        rows = []
        for k in range(STEP // LANES):
            part = hidden_ref[:, pl.ds(pl.multiple_of(at + k * LANES, LANES), LANES)].astype(jnp.float32)
            gain = gain_ref[pl.ds(m * (STEP // LANES) + k, 1), :]
            rows.append((part * inv * gain).astype(jnp.bfloat16))
        return key + jnp.dot(jnp.concatenate(rows, axis=1), weight, preferred_element_type=jnp.float32)

    key = lax.fori_loop(
        0, width // STEP, forward, jnp.zeros(key_ref.shape, jnp.float32), unroll=2
    )
    key_ref[...] = key.astype(jnp.bfloat16)
    cot = cot_ref[...]
    scale = inv * (jnp.sum(cot.astype(jnp.float32) * key, axis=1, keepdims=True) / width)

    def backward(m, _):
        at = pl.multiple_of(m * STEP, STEP)
        back = lax.dot_general(
            cot, w_ref[pl.ds(at, STEP), :], (((1,), (1,)), ((), ())), preferred_element_type=jnp.float32
        )
        for k in range(STEP // LANES):
            lanes = pl.ds(pl.multiple_of(at + k * LANES, LANES), LANES)
            part = hidden_ref[:, lanes].astype(jnp.float32)
            gain = gain_ref[pl.ds(m * (STEP // LANES) + k, 1), :]
            grad = inv * (back[:, k * LANES : (k + 1) * LANES] * gain - part * scale)
            grad_ref[:, lanes] = grad.astype(jnp.bfloat16)
        return 0

    lax.fori_loop(0, width // STEP, backward, 0, unroll=2)


def local(hidden_in, cotangent, params):
    tokens, width = hidden_in.shape
    x, c, z = lax.axis_index("x"), lax.axis_index("c"), lax.axis_index("z")
    yh, yl = lax.axis_index("yh"), lax.axis_index("yl")
    inner, j = (z * 2 + yl) * 4 + x, yh * 2 + c
    row0, lane = first_row(yh, c), (96 * j) % LANES
    pos = jnp.stack([x, c]).astype(jnp.int32)
    smem = pl.BlockSpec(memory_space=pltpu.SMEM)
    vmem = pl.BlockSpec(memory_space=pltpu.VMEM)
    bf16, f32 = jnp.bfloat16, jnp.float32

    flat = jnp.pad(params.reshape(-1), (LANES, BLK * LANES - PIECE))
    block = lax.dynamic_slice(flat, (LANES - lane,), (BLK * LANES,)).reshape(1, BLK, LANES)
    mine = lax.all_to_all(jnp.broadcast_to(block, (N_ZY, BLK, LANES)), ZY, 0, 0, tiled=True)

    half = jax.ShapeDtypeStruct((4, N_ZY, BLK, LANES), bf16)
    own, send, inv = pl.pallas_call(
        sums_kernel,
        out_shape=(half, half, jax.ShapeDtypeStruct((tokens, LANES), f32)),
        in_specs=[smem, vmem, vmem],
        out_specs=(vmem, vmem, vmem),
        scratch_shapes=[pltpu.VMEM((ROWS_PAD, LANES), f32)],
        compiler_params=pltpu.CompilerParams(vmem_limit_bytes=24 << 20),
        cost_estimate=pl.CostEstimate(flops=4 * tokens * width * LANES, bytes_accessed=8 << 20, transcendentals=0),
    )(pos, hidden_in, cotangent)
    got = swap(send)
    moved = {}
    for k in (2, 1, 3):
        sent, got = lax.optimization_barrier(((own[k].astype(f32) + got[k].astype(f32)).astype(bf16), got))
        moved[k] = shift_x(sent, k)
    moved[2], mine = lax.optimization_barrier((moved[2], mine))
    held = [mine] + [shift_x(mine, k) for k in range(1, 4)]
    other = [swap(mine), swap(jnp.stack(held[1:]))]


    total = own[0].astype(f32) + got[0].astype(f32)
    total = total + moved[1].astype(f32) + moved[2].astype(f32) + moved[3].astype(f32)
    gain_part = jnp.sum(mine.astype(f32) * total, axis=-1)[:, :USED].reshape(12, 8 * USED)
    pays = [jnp.zeros((512,), f32)]
    for start in (0, 3, 7):
        pays.append(jnp.pad(gain_part[start : start + 5].reshape(-1), (0, 32)))
    pay = jnp.stack(pays).reshape(4, 1, 4, LANES)
    pay = jnp.concatenate([jnp.zeros_like(pay), pay], axis=1).reshape(8, 4, LANES)
    pay = jnp.pad(pay, ((N_ZY - 8, 0), (USED, 0), (0, 0)))
    spare = lax.broadcasted_iota(jnp.int32, (1, BLK, 1), 1) >= USED
    chunk = jnp.where(spare, pay, total).astype(bf16)
    received = lax.all_to_all(chunk, ZY, 0, 0, tiled=True)

    key_rows, input_grad, gains = pl.pallas_call(
        rows_kernel,
        out_shape=(
            jax.ShapeDtypeStruct((tokens, LANES), bf16),
            jax.ShapeDtypeStruct((tokens, width), bf16),
            jax.ShapeDtypeStruct((64, LANES), f32),
        ),
        in_specs=[smem] + [vmem] * 9,
        out_specs=(vmem, vmem, vmem),
        scratch_shapes=[pltpu.VMEM((2, ROWS_PAD, LANES), f32), pltpu.VMEM((width, LANES), bf16)],
        compiler_params=pltpu.CompilerParams(vmem_limit_bytes=36 << 20),
        cost_estimate=pl.CostEstimate(flops=4 * tokens * width * LANES, bytes_accessed=10 << 20, transcendentals=0),
    )(pos, hidden_in, cotangent, inv, *held, *other)

    sums = received.astype(f32).sum(axis=0)
    part = sums[USED:]
    parts = lax.all_to_all(jnp.broadcast_to(part, (8, 4, LANES)), ("c", "x"), 0, 0, tiled=True)
    parts, gains = lax.optimization_barrier((parts, gains))
    both = parts.reshape(2, 4, 512)[:, :, :480].reshape(2, 4, 5, 4, 2, USED)
    by_row = 0.0
    for core in range(2):
        for hi in range(4):
            at = (43 * (2 * hi + core)) // 4
            by_row = by_row + jnp.pad(both[core, :, :, hi], ((0, 0), (0, 0), (0, 0), (at, 88 - USED - at)))
    by_row = by_row[..., :GROUP_ROWS].transpose(1, 2, 0, 3).reshape(-1)
    start = jnp.where(yh == 2, 3, jnp.where(yh == 3, 7, 0)) * 688
    gain_grad = lax.dynamic_slice(jnp.pad(by_row, (2816, 0)), (PIECE * j - start,), (PIECE,))

    row_gain = lax.dynamic_slice(jnp.pad(gains.reshape(-1), (0, 80)), (GROUP_ROWS * inner + row0,), (USED,))
    weight_grad = (sums[:USED] * row_gain[:, None]).reshape(-1)
    weight_grad = lax.dynamic_slice(weight_grad, (lane,), (PIECE,))
    param_grad = weight_grad + jnp.where(inner == 95, gain_grad, 0.0)
    return (key_rows, input_grad, param_grad.reshape(1, PIECE))


def solution(mesh):
    fine = Mesh(mesh.devices.reshape(SIZES), AXES)
    tokens = P(AXES, None)
    params = P(("z", "yl", "x"), ("yh", "c"))
    return jax.shard_map(
        local, mesh=fine, in_specs=(tokens, tokens, params), out_specs=(tokens, tokens, params), check_vma=False
    )
```

```python
import jax
import jax.numpy as jnp
from jax import lax
from jax.experimental import pallas as pl
from jax.experimental.pallas import tpu as pltpu
from jax.sharding import Mesh, PartitionSpec as P

AXES = ("yh", "c", "z", "yl", "x")
SIZES = (4, 2, 12, 2, 4)
ZY = ("z", "yh", "yl")
N_ZY = 96

LANES = 128
BLK = 16
USED = 12
GROUP_ROWS = 86
PIECE = 1376
EPS = 1e-05
ROWS_PAD = 8272
STEP = 1024


def swap(a):
    return lax.ppermute(a, "c", [(0, 1), (1, 0)])


def shift_x(a, k):
    return lax.ppermute(a, "x", [(i, (i + k) % 4) for i in range(4)])


def first_row(yh, core):
    return lax.div(43 * (2 * yh + core), 4)


def sums_kernel(pos_ref, hidden_ref, cot_ref, own_ref, send_ref, inv_ref, u_ref):
    width = hidden_ref.shape[1]
    x, c = pos_ref[0], pos_ref[1]

    def squares(m, acc):
        part = hidden_ref[:, pl.ds(pl.multiple_of(m * STEP, STEP), STEP)].astype(jnp.float32)
        part = part * part
        for k in range(STEP // LANES):
            acc = acc + part[:, k * LANES : (k + 1) * LANES]
        return acc

    zero = jnp.zeros((hidden_ref.shape[0], LANES), jnp.float32)
    acc = lax.fori_loop(0, width // STEP, squares, zero, unroll=2)
    inv = lax.rsqrt(jnp.sum(acc, axis=1, keepdims=True) / width + EPS)
    inv_ref[...] = jnp.broadcast_to(inv, inv_ref.shape)
    cots = (cot_ref[...].astype(jnp.float32) * inv).astype(jnp.bfloat16)

    def outer(m, _):
        at = pl.multiple_of(m * STEP, STEP)
        u_ref[pl.ds(at, STEP), :] = lax.dot_general(
            hidden_ref[:, pl.ds(at, STEP)], cots, (((0,), (0,)), ((), ())), preferred_element_type=jnp.float32
        )
        return 0

    lax.fori_loop(0, width // STEP, outer, 0, unroll=4)
    u_ref[width:, :] = jnp.zeros((ROWS_PAD - width, LANES), jnp.float32)

    starts = [[GROUP_ROWS * lax.rem(x + k, 4) + first_row(yh, core) for yh in range(4)] for core in (c, 1 - c) for k in range(4)]

    def pack(q, _):
        place = (q // 2) * 8 + lax.rem(q, 2)
        base = 4 * GROUP_ROWS * q
        for side, out in enumerate((own_ref, send_ref)):
            for k in range(4):
                for yh in range(4):
                    row = base + starts[4 * side + k][yh]
                    out[k, place + 2 * yh] = u_ref[pl.ds(row, BLK), :].astype(jnp.bfloat16)
        return 0

    lax.fori_loop(0, 24, pack, 0, unroll=2)


def rows_kernel(pos_ref, hidden_ref, cot_ref, inv_ref, *refs):
    key_ref, grad_ref, gain_ref, s_ref, w_ref = refs[6:]
    pieces = (refs[:4], [refs[4]] + [refs[5].at[k] for k in range(3)])
    width = hidden_ref.shape[1]
    x, c = pos_ref[0], pos_ref[1]

    s_ref[1, 0:BLK, :] = jnp.zeros((BLK, LANES), jnp.float32)
    tail = jnp.zeros((22 - BLK, LANES), jnp.float32)
    one = jnp.zeros((1, LANES), jnp.float32)

    offsets = [[first_row(yh, core) for yh in range(4)] for core in (c, 1 - c)]
    bases = [GROUP_ROWS * lax.rem(x + 4 - k, 4) for k in range(4)]

    def assemble(q, _):
        place = (q // 2) * 8 + lax.rem(q, 2)
        for k in range(4):
            base = 4 * GROUP_ROWS * q + bases[k]
            for side, core in enumerate((c, 1 - c)):
                s_ref[core, pl.ds(base + 85, 1), :] = one
                for yh in range(4):
                    row = base + offsets[side][yh]
                    s_ref[core, pl.ds(row, BLK), :] = pieces[side][k][place + 2 * yh].astype(jnp.float32)
                    rest = 6 if yh < 3 else 5
                    s_ref[core, pl.ds(row + BLK, rest), :] = tail[:rest]
        return 0

    lax.fori_loop(0, 24, assemble, 0, unroll=2)
    gain_ref[...] = s_ref[0, width : width + 64, :] + s_ref[1, width : width + 64, :]
    inv = inv_ref[...]

    def forward(m, key):
        at = pl.multiple_of(m * STEP, STEP)
        weight = (s_ref[0, pl.ds(at, STEP), :] + s_ref[1, pl.ds(at, STEP), :]).astype(jnp.bfloat16)
        w_ref[pl.ds(at, STEP), :] = weight
        rows = []
        for k in range(STEP // LANES):
            part = hidden_ref[:, pl.ds(pl.multiple_of(at + k * LANES, LANES), LANES)].astype(jnp.float32)
            gain = gain_ref[pl.ds(m * (STEP // LANES) + k, 1), :]
            rows.append((part * inv * gain).astype(jnp.bfloat16))
        return key + jnp.dot(jnp.concatenate(rows, axis=1), weight, preferred_element_type=jnp.float32)

    key = lax.fori_loop(
        0, width // STEP, forward, jnp.zeros(key_ref.shape, jnp.float32), unroll=4
    )
    key_ref[...] = key.astype(jnp.bfloat16)
    cot = cot_ref[...]
    scale = inv * (jnp.sum(cot.astype(jnp.float32) * key, axis=1, keepdims=True) / width)

    def backward(m, _):
        at = pl.multiple_of(m * STEP, STEP)
        back = lax.dot_general(
            cot, w_ref[pl.ds(at, STEP), :], (((1,), (1,)), ((), ())), preferred_element_type=jnp.float32
        )
        for k in range(STEP // LANES):
            lanes = pl.ds(pl.multiple_of(at + k * LANES, LANES), LANES)
            part = hidden_ref[:, lanes].astype(jnp.float32)
            gain = gain_ref[pl.ds(m * (STEP // LANES) + k, 1), :]
            grad = inv * (back[:, k * LANES : (k + 1) * LANES] * gain - part * scale)
            grad_ref[:, lanes] = grad.astype(jnp.bfloat16)
        return 0

    lax.fori_loop(0, width // STEP, backward, 0, unroll=4)


def local(hidden_in, cotangent, params):
    tokens, width = hidden_in.shape
    x, c, z = lax.axis_index("x"), lax.axis_index("c"), lax.axis_index("z")
    yh, yl = lax.axis_index("yh"), lax.axis_index("yl")
    inner, j = (z * 2 + yl) * 4 + x, yh * 2 + c
    row0, lane = first_row(yh, c), (96 * j) % LANES
    pos = jnp.stack([x, c]).astype(jnp.int32)
    smem = pl.BlockSpec(memory_space=pltpu.SMEM)
    vmem = pl.BlockSpec(memory_space=pltpu.VMEM)
    bf16, f32 = jnp.bfloat16, jnp.float32

    flat = jnp.pad(params.reshape(-1), (LANES, BLK * LANES - PIECE))
    block = lax.dynamic_slice(flat, (LANES - lane,), (BLK * LANES,)).reshape(1, BLK, LANES)
    mine = lax.all_to_all(jnp.broadcast_to(block, (N_ZY, BLK, LANES)), ZY, 0, 0, tiled=True)

    half = jax.ShapeDtypeStruct((4, N_ZY, BLK, LANES), bf16)
    own, send, inv = pl.pallas_call(
        sums_kernel,
        out_shape=(half, half, jax.ShapeDtypeStruct((tokens, LANES), f32)),
        in_specs=[smem, vmem, vmem],
        out_specs=(vmem, vmem, vmem),
        scratch_shapes=[pltpu.VMEM((ROWS_PAD, LANES), f32)],
        compiler_params=pltpu.CompilerParams(vmem_limit_bytes=24 << 20),
        cost_estimate=pl.CostEstimate(flops=4 * tokens * width * LANES, bytes_accessed=8 << 20, transcendentals=0),
    )(pos, hidden_in, cotangent)
    got = swap(send)
    moved = {}
    for k in (2, 1, 3):
        sent, got = lax.optimization_barrier(((own[k].astype(f32) + got[k].astype(f32)).astype(bf16), got))
        moved[k] = shift_x(sent, k)
    moved[2], mine = lax.optimization_barrier((moved[2], mine))
    held = [mine] + [shift_x(mine, k) for k in range(1, 4)]
    other = [swap(mine), swap(jnp.stack(held[1:]))]


    total = own[0].astype(f32) + got[0].astype(f32)
    total = total + moved[1].astype(f32) + moved[2].astype(f32) + moved[3].astype(f32)
    products = jnp.sum(mine.astype(f32) * total, axis=-1)
    products, total = lax.optimization_barrier((products, total.astype(bf16)))
    gain_part = products[:, :USED].reshape(12, 8 * USED)
    pays = [jnp.zeros((512,), f32)]
    for start in (0, 3, 7):
        pays.append(jnp.pad(gain_part[start : start + 5].reshape(-1), (0, 32)))
    pay = jnp.stack(pays).reshape(4, 1, 4, LANES)
    pay = jnp.concatenate([jnp.zeros_like(pay), pay], axis=1).reshape(8, 4, LANES)
    pay = jnp.pad(pay, ((N_ZY - 8, 0), (USED, 0), (0, 0)))
    spare = lax.broadcasted_iota(jnp.int32, (1, BLK, 1), 1) >= USED
    chunk = jnp.where(spare, pay.astype(bf16), total)
    received = lax.all_to_all(chunk, ZY, 0, 0, tiled=True)

    key_rows, input_grad, gains = pl.pallas_call(
        rows_kernel,
        out_shape=(
            jax.ShapeDtypeStruct((tokens, LANES), bf16),
            jax.ShapeDtypeStruct((tokens, width), bf16),
            jax.ShapeDtypeStruct((64, LANES), f32),
        ),
        in_specs=[smem] + [vmem] * 9,
        out_specs=(vmem, vmem, vmem),
        scratch_shapes=[pltpu.VMEM((2, ROWS_PAD, LANES), f32), pltpu.VMEM((width, LANES), bf16)],
        compiler_params=pltpu.CompilerParams(vmem_limit_bytes=36 << 20),
        cost_estimate=pl.CostEstimate(flops=4 * tokens * width * LANES, bytes_accessed=10 << 20, transcendentals=0),
    )(pos, hidden_in, cotangent, inv, *held, *other)

    sums = received.astype(f32).sum(axis=0)
    part = sums[USED:]
    parts = lax.all_to_all(jnp.broadcast_to(part, (8, 4, LANES)), ("c", "x"), 0, 0, tiled=True)
    parts, gains = lax.optimization_barrier((parts, gains))
    both = parts.reshape(2, 4, 512)[:, :, :480].reshape(2, 4, 5, 4, 2, USED)
    by_row = 0.0
    for core in range(2):
        for hi in range(4):
            at = (43 * (2 * hi + core)) // 4
            by_row = by_row + jnp.pad(both[core, :, :, hi], ((0, 0), (0, 0), (0, 0), (at, 88 - USED - at)))
    by_row = by_row[..., :GROUP_ROWS].transpose(1, 2, 0, 3).reshape(-1)
    start = jnp.where(yh == 2, 3, jnp.where(yh == 3, 7, 0)) * 688
    gain_grad = lax.dynamic_slice(jnp.pad(by_row, (2816, 0)), (PIECE * j - start,), (PIECE,))

    row_gain = lax.dynamic_slice(jnp.pad(gains.reshape(-1), (0, 80)), (GROUP_ROWS * inner + row0,), (USED,))
    weight_grad = (sums[:USED] * row_gain[:, None]).reshape(-1)
    weight_grad = lax.dynamic_slice(weight_grad, (lane,), (PIECE,))
    param_grad = weight_grad + jnp.where(inner == 95, gain_grad, 0.0)
    return (key_rows, input_grad, param_grad.reshape(1, PIECE))


def solution(mesh):
    fine = Mesh(mesh.devices.reshape(SIZES), AXES)
    tokens = P(AXES, None)
    params = P(("z", "yl", "x"), ("yh", "c"))
    return jax.shard_map(
        local, mesh=fine, in_specs=(tokens, tokens, params), out_specs=(tokens, tokens, params), check_vma=False
    )
```

```python
import jax
import jax.numpy as jnp
from jax import lax
from jax.experimental import pallas as pl
from jax.experimental.pallas import tpu as pltpu
from jax.sharding import Mesh, PartitionSpec as P

AXES = ("yh", "c", "z", "yl", "x")
SIZES = (4, 2, 12, 2, 4)
ZY = ("z", "yh", "yl")
N_ZY = 96

LANES = 128
BLK = 16
USED = 12
GROUP_ROWS = 86
PIECE = 1376
EPS = 1e-05
ROWS_PAD = 8272
STEP = 1024


def swap(a):
    return lax.ppermute(a, "c", [(0, 1), (1, 0)])


def shift_x(a, k):
    return lax.ppermute(a, "x", [(i, (i + k) % 4) for i in range(4)])


def first_row(yh, core):
    return lax.div(43 * (2 * yh + core), 4)


def sums_kernel(pos_ref, hidden_hbm, cot_hbm, own_ref, send_ref, inv_ref, u_ref, hidden_ref, cot_ref, sems):
    width = hidden_ref.shape[1]
    x, c = pos_ref[0], pos_ref[1]
    quarter = width // 4
    copies = []
    for k in range(4):
        lanes = pl.ds(k * quarter, quarter)
        copies.append(pltpu.make_async_copy(hidden_hbm.at[:, lanes], hidden_ref.at[:, lanes], sems.at[k]))
    copies.append(pltpu.make_async_copy(cot_hbm, cot_ref, sems.at[4]))
    for copy in copies:
        copy.start()

    def squares(m, acc):
        part = hidden_ref[:, pl.ds(pl.multiple_of(m * STEP, STEP), STEP)].astype(jnp.float32)
        part = part * part
        for k in range(STEP // LANES):
            acc = acc + part[:, k * LANES : (k + 1) * LANES]
        return acc

    acc = jnp.zeros((hidden_ref.shape[0], LANES), jnp.float32)
    for k in range(4):
        copies[k].wait()
        acc = lax.fori_loop(k * quarter // STEP, (k + 1) * quarter // STEP, squares, acc, unroll=True)
    copies[4].wait()
    inv = lax.rsqrt(jnp.sum(acc, axis=1, keepdims=True) / width + EPS)
    inv_ref[...] = jnp.broadcast_to(inv, inv_ref.shape)
    cots = (cot_ref[...].astype(jnp.float32) * inv).astype(jnp.bfloat16)

    def outer(m, _):
        at = pl.multiple_of(m * STEP, STEP)
        u_ref[pl.ds(at, STEP), :] = lax.dot_general(
            hidden_ref[:, pl.ds(at, STEP)], cots, (((0,), (0,)), ((), ())), preferred_element_type=jnp.float32
        )
        return 0

    lax.fori_loop(0, width // STEP, outer, 0, unroll=4)
    u_ref[width:, :] = jnp.zeros((ROWS_PAD - width, LANES), jnp.float32)

    starts = [[GROUP_ROWS * lax.rem(x + k, 4) + first_row(yh, core) for yh in range(4)] for core in (c, 1 - c) for k in range(4)]

    def pack(q, _):
        place = (q // 2) * 8 + lax.rem(q, 2)
        base = 4 * GROUP_ROWS * q
        for side, out in enumerate((own_ref, send_ref)):
            for k in range(4):
                for yh in range(4):
                    row = base + starts[4 * side + k][yh]
                    out[k, place + 2 * yh] = u_ref[pl.ds(row, BLK), :].astype(jnp.bfloat16)
        return 0

    lax.fori_loop(0, 24, pack, 0, unroll=2)


def rows_kernel(pos_ref, hidden_ref, cot_ref, inv_ref, *refs):
    key_ref, grad_ref, gain_ref, s_ref, w_ref = refs[6:]
    pieces = (refs[:4], [refs[4]] + [refs[5].at[k] for k in range(3)])
    width = hidden_ref.shape[1]
    x, c = pos_ref[0], pos_ref[1]

    s_ref[1, 0:BLK, :] = jnp.zeros((BLK, LANES), jnp.float32)
    tail = jnp.zeros((22 - BLK, LANES), jnp.float32)
    one = jnp.zeros((1, LANES), jnp.float32)

    offsets = [[first_row(yh, core) for yh in range(4)] for core in (c, 1 - c)]
    bases = [GROUP_ROWS * lax.rem(x + 4 - k, 4) for k in range(4)]

    def assemble(q, _):
        place = (q // 2) * 8 + lax.rem(q, 2)
        for k in range(4):
            base = 4 * GROUP_ROWS * q + bases[k]
            for side, core in enumerate((c, 1 - c)):
                s_ref[core, pl.ds(base + 85, 1), :] = one
                for yh in range(4):
                    row = base + offsets[side][yh]
                    s_ref[core, pl.ds(row, BLK), :] = pieces[side][k][place + 2 * yh].astype(jnp.float32)
                    rest = 6 if yh < 3 else 5
                    s_ref[core, pl.ds(row + BLK, rest), :] = tail[:rest]
        return 0

    lax.fori_loop(0, 24, assemble, 0, unroll=2)
    gain_ref[...] = s_ref[0, width : width + 64, :] + s_ref[1, width : width + 64, :]
    inv = inv_ref[...]

    def forward(m, key):
        at = pl.multiple_of(m * STEP, STEP)
        weight = (s_ref[0, pl.ds(at, STEP), :] + s_ref[1, pl.ds(at, STEP), :]).astype(jnp.bfloat16)
        w_ref[pl.ds(at, STEP), :] = weight
        rows = []
        for k in range(STEP // LANES):
            part = hidden_ref[:, pl.ds(pl.multiple_of(at + k * LANES, LANES), LANES)].astype(jnp.float32)
            gain = gain_ref[pl.ds(m * (STEP // LANES) + k, 1), :]
            rows.append((part * inv * gain).astype(jnp.bfloat16))
        return key + jnp.dot(jnp.concatenate(rows, axis=1), weight, preferred_element_type=jnp.float32)

    key = lax.fori_loop(
        0, width // STEP, forward, jnp.zeros(key_ref.shape, jnp.float32), unroll=4
    )
    key_ref[...] = key.astype(jnp.bfloat16)
    cot = cot_ref[...]
    scale = inv * (jnp.sum(cot.astype(jnp.float32) * key, axis=1, keepdims=True) / width)

    def backward(m, _):
        at = pl.multiple_of(m * STEP, STEP)
        back = lax.dot_general(
            cot, w_ref[pl.ds(at, STEP), :], (((1,), (1,)), ((), ())), preferred_element_type=jnp.float32
        )
        for k in range(STEP // LANES):
            lanes = pl.ds(pl.multiple_of(at + k * LANES, LANES), LANES)
            part = hidden_ref[:, lanes].astype(jnp.float32)
            gain = gain_ref[pl.ds(m * (STEP // LANES) + k, 1), :]
            grad = inv * (back[:, k * LANES : (k + 1) * LANES] * gain - part * scale)
            grad_ref[:, lanes] = grad.astype(jnp.bfloat16)
        return 0

    lax.fori_loop(0, width // STEP, backward, 0, unroll=4)


def local(hidden_in, cotangent, params):
    tokens, width = hidden_in.shape
    x, c, z = lax.axis_index("x"), lax.axis_index("c"), lax.axis_index("z")
    yh, yl = lax.axis_index("yh"), lax.axis_index("yl")
    inner, j = (z * 2 + yl) * 4 + x, yh * 2 + c
    row0, lane = first_row(yh, c), (96 * j) % LANES
    pos = jnp.stack([x, c]).astype(jnp.int32)
    smem = pl.BlockSpec(memory_space=pltpu.SMEM)
    vmem = pl.BlockSpec(memory_space=pltpu.VMEM)
    bf16, f32 = jnp.bfloat16, jnp.float32

    flat = jnp.pad(params.reshape(-1), (LANES, BLK * LANES - PIECE))
    block = lax.dynamic_slice(flat, (LANES - lane,), (BLK * LANES,)).reshape(1, BLK, LANES)
    mine = lax.all_to_all(jnp.broadcast_to(block, (N_ZY, BLK, LANES)), ZY, 0, 0, tiled=True)

    half = jax.ShapeDtypeStruct((4, N_ZY, BLK, LANES), bf16)
    own, send, inv = pl.pallas_call(
        sums_kernel,
        out_shape=(half, half, jax.ShapeDtypeStruct((tokens, LANES), f32)),
        in_specs=[smem, pl.BlockSpec(memory_space=pl.ANY), pl.BlockSpec(memory_space=pl.ANY)],
        out_specs=(vmem, vmem, vmem),
        scratch_shapes=[
            pltpu.VMEM((ROWS_PAD, LANES), f32),
            pltpu.VMEM((tokens, width), bf16),
            pltpu.VMEM((tokens, LANES), bf16),
            pltpu.SemaphoreType.DMA((5,)),
        ],
        compiler_params=pltpu.CompilerParams(vmem_limit_bytes=60 << 20),
        cost_estimate=pl.CostEstimate(flops=4 * tokens * width * LANES, bytes_accessed=8 << 20, transcendentals=0),
    )(pos, hidden_in, cotangent)
    got = swap(send)
    moved = {}
    for k in (2, 1, 3):
        sent, got = lax.optimization_barrier(((own[k].astype(f32) + got[k].astype(f32)).astype(bf16), got))
        moved[k] = shift_x(sent, k)
    moved[2], mine = lax.optimization_barrier((moved[2], mine))
    held = [mine] + [shift_x(mine, k) for k in range(1, 4)]
    other = [swap(mine), swap(jnp.stack(held[1:]))]


    total = own[0].astype(f32) + got[0].astype(f32)
    total = total + moved[1].astype(f32) + moved[2].astype(f32) + moved[3].astype(f32)
    products = jnp.sum(mine.astype(f32) * total, axis=-1)
    products, total = lax.optimization_barrier((products, total.astype(bf16)))
    gain_part = products[:, :USED].reshape(12, 8 * USED)
    pays = [jnp.zeros((512,), f32)]
    for start in (0, 3, 7):
        pays.append(jnp.pad(gain_part[start : start + 5].reshape(-1), (0, 32)))
    pay = jnp.stack(pays).reshape(4, 1, 4, LANES)
    pay = jnp.concatenate([jnp.zeros_like(pay), pay], axis=1).reshape(8, 4, LANES)
    pay = jnp.pad(pay, ((N_ZY - 8, 0), (USED, 0), (0, 0)))
    spare = lax.broadcasted_iota(jnp.int32, (1, BLK, 1), 1) >= USED
    chunk = jnp.where(spare, pay.astype(bf16), total)
    received = lax.all_to_all(chunk, ZY, 0, 0, tiled=True)

    key_rows, input_grad, gains = pl.pallas_call(
        rows_kernel,
        out_shape=(
            jax.ShapeDtypeStruct((tokens, LANES), bf16),
            jax.ShapeDtypeStruct((tokens, width), bf16),
            jax.ShapeDtypeStruct((64, LANES), f32),
        ),
        in_specs=[smem] + [vmem] * 9,
        out_specs=(vmem, vmem, vmem),
        scratch_shapes=[pltpu.VMEM((2, ROWS_PAD, LANES), f32), pltpu.VMEM((width, LANES), bf16)],
        compiler_params=pltpu.CompilerParams(vmem_limit_bytes=36 << 20),
        cost_estimate=pl.CostEstimate(flops=4 * tokens * width * LANES, bytes_accessed=10 << 20, transcendentals=0),
    )(pos, hidden_in, cotangent, inv, *held, *other)

    sums = received.astype(f32).sum(axis=0)
    part = sums[USED:]
    parts = lax.all_to_all(jnp.broadcast_to(part, (8, 4, LANES)), ("c", "x"), 0, 0, tiled=True)
    parts, gains = lax.optimization_barrier((parts, gains))
    both = parts.reshape(2, 4, 512)[:, :, :480].reshape(2, 4, 5, 4, 2, USED)
    by_row = 0.0
    for core in range(2):
        for hi in range(4):
            at = (43 * (2 * hi + core)) // 4
            by_row = by_row + jnp.pad(both[core, :, :, hi], ((0, 0), (0, 0), (0, 0), (at, 88 - USED - at)))
    by_row = by_row[..., :GROUP_ROWS].transpose(1, 2, 0, 3).reshape(-1)
    start = jnp.where(yh == 2, 3, jnp.where(yh == 3, 7, 0)) * 688
    gain_grad = lax.dynamic_slice(jnp.pad(by_row, (2816, 0)), (PIECE * j - start,), (PIECE,))

    row_gain = lax.dynamic_slice(jnp.pad(gains.reshape(-1), (0, 80)), (GROUP_ROWS * inner + row0,), (USED,))
    weight_grad = (sums[:USED] * row_gain[:, None]).reshape(-1)
    weight_grad = lax.dynamic_slice(weight_grad, (lane,), (PIECE,))
    param_grad = weight_grad + jnp.where(inner == 95, gain_grad, 0.0)
    return (key_rows, input_grad, param_grad.reshape(1, PIECE))


def solution(mesh):
    fine = Mesh(mesh.devices.reshape(SIZES), AXES)
    tokens = P(AXES, None)
    params = P(("z", "yl", "x"), ("yh", "c"))
    return jax.shard_map(
        local, mesh=fine, in_specs=(tokens, tokens, params), out_specs=(tokens, tokens, params), check_vma=False
    )
```
